256 devices in a mesh: row: 16 (over z_lo, x, core), col: 16 (over z_hi, y).
Axes of the slice: x: 4, y: 4, z: 8 (z_hi: 4, z_lo: 2; z = z_hi * 2 + z_lo), core: 2. Of those that a mesh axis runs over, the one named last changes fastest.
Arguments:
- residual: bfloat16 [30720, 512], P('row', 'col'), may hold values from -4 to 4
- interaction: bfloat16 [30720, 5120], P('row', 'col'), may hold values from -0.078125 to 0.078125
- commands: bfloat16 [5120, 512], P('col'), may hold values from -6 to 6
- slope_valid: int32 [240], P('row'), may hold values 0 or 1
- frame_valid: int32 [512], P('col'), may hold values 0 or 1
Outputs:
- covariance: bfloat16 [30720, 30720], P('row', 'col')
The draws below stay inside these ranges and needn't reach their ends.
All inputs are finite; a program needn't handle non-finite values. No bound on the sum of `slope_valid` or of `frame_valid` on one device may be relied on, other than what follows from the above.
Results may differ from the reference program's by a relative error of at most 0.02.
Values may be sent and summed in bfloat16 or wider, within the bound.
No kernel may reach another device: no remote copies, remote signals or barrier semaphores. Data moves between devices by JAX's collectives and lax.ppermute only.
A program may use at most 64 MiB of HBM per device.

```python
import jax
import jax.numpy as jnp
from jax import lax

NS = 30720
NA = 5120
SBLK = 128
FRAMES = 512
NSB = 240
N_ROW = 16
N_COL = 16


def touch_ends(values, stream_key, least, high):
    longest = values.shape.index(max(values.shape))
    spots = []
    for shift in (0, 1):
        where = [jax.random.randint(jax.random.fold_in(stream_key, axis), (), 0, length) for axis, length in enumerate(values.shape)]
        where[longest] = (where[longest] + shift) % values.shape[longest]
        spots.append(tuple(where))
    return values.at[spots[0]].set(least).at[spots[1]].set(high)


def steps_of(stream_key, extent, shards, least, largest):
    loudness = 1.0
    for axis_at, parts in shards:
        steps = jax.random.uniform(jax.random.fold_in(jax.random.fold_in(stream_key, 6), axis_at), (parts,), jnp.float32, least / len(shards), largest / len(shards))
        loudness = loudness * jnp.repeat(jnp.exp(steps), extent[axis_at] // parts).reshape((-1,) + (1,) * (len(extent) - 1 - axis_at))
    return loudness


def normal_values(rng, extent, scale, reach, pieces=(), held_as=jnp.bfloat16):
    result = jax.random.normal(rng, extent, jnp.float32) * scale
    if len(pieces) > 0:
        result = steps_of(rng, extent, pieces, -0.22, 0.18) * result
    return jnp.clip(result, min=-reach, max=reach).astype(held_as)


def setup_inputs(seed: int = 0) -> dict:
    arg_keys = jax.random.split(jax.random.key(seed), 6)
    residual = normal_values(arg_keys[0], (NS, FRAMES), 0.5, 4.0, ((0, 16), (1, 16)))
    interaction = normal_values(arg_keys[1], (NS, NA), NA ** -0.5, 0.078125, ((0, 16), (1, 16)))
    commands = normal_values(arg_keys[2], (NA, FRAMES), 1.0, 6.0, ((0, 16),))
    slope_valid = touch_ends((jax.random.randint(arg_keys[3], (NSB,), 0, 8) < 7).astype(jnp.int32), jax.random.fold_in(arg_keys[3], 1), 0, 1)
    frame_valid = touch_ends((jax.random.randint(arg_keys[4], (FRAMES,), 0, 8) < 7).astype(jnp.int32), jax.random.fold_in(arg_keys[4], 1), 0, 1)
    return dict(residual=residual, interaction=interaction, commands=commands, slope_valid=slope_valid, frame_valid=frame_valid)


def reference(residual, interaction, commands, slope_valid, frame_valid):
    width = NA // N_COL
    total = residual.astype(jnp.float32)
    for block in range(N_COL):
        term = jnp.dot(interaction[:, block * width:(block + 1) * width], commands[block * width:(block + 1) * width, :], preferred_element_type=jnp.float32)
        rounded = lax.optimization_barrier(term.astype(jnp.bfloat16))
        total = total + rounded.astype(jnp.float32)
    row_mask = (slope_valid[:, None] * jnp.ones((1, SBLK), jnp.int32)).reshape(-1).astype(jnp.float32)
    slopes = (total * row_mask[:, None] * frame_valid[None, :].astype(jnp.float32)).astype(jnp.bfloat16)
    block_rows = NS // N_ROW
    blocks = slopes.reshape(N_ROW, block_rows, FRAMES)
    starts = jnp.arange(N_ROW, dtype=jnp.int32) * block_rows

    def one_block(inputs):
        chosen, start = inputs
        tile = jnp.dot(chosen, slopes.T, preferred_element_type=jnp.float32) / FRAMES
        row_ids = start + jnp.arange(block_rows, dtype=jnp.int32)[:, None]
        col_ids = jnp.arange(NS, dtype=jnp.int32)[None, :]
        return jnp.where(row_ids <= col_ids, tile, jnp.float32(0.0)).astype(jnp.bfloat16)

    return lax.map(one_block, (blocks, starts)).reshape(NS, NS)
```

```python
import jax
import jax.numpy as jnp
from jax import lax
from jax.sharding import PartitionSpec as P

SBLK = 128
FRAMES = 512
MASKS_A = (0, 3, 1, 2)
MASKS_B = (0, 1, 3, 2)


def y_swap(mask):
    return [(c, c ^ mask) for c in range(16)]


def z_swap(mask):
    return [(c, c ^ (4 * mask)) for c in range(16)]


def y_turn(by):
    return [(c, (c & 12) | ((c + by) & 3)) for c in range(16)]


def z_turn(by):
    return [(c, (c + 4 * by) & 15) for c in range(16)]


def x_turn(by):
    return [(r, (r & 9) | ((r + 2 * by) & 6)) for r in range(16)]


def add(one, other):
    return (one.astype(jnp.float32) + other.astype(jnp.float32)).astype(jnp.bfloat16)


def ring_gather(own, axis, turn):
    half = own.shape[0] // 2
    left = lax.ppermute(own, axis, turn(1))
    right = lax.ppermute(own, axis, turn(-1))
    far_a = lax.ppermute(left[:half], axis, turn(1))
    far_b = lax.ppermute(right[half:], axis, turn(-1))
    return jnp.concatenate([own, left, right, far_a, far_b], axis=0)


def frame_order(col):
    half, y_at, z_at, low = jnp.meshgrid(
        jnp.arange(2), jnp.arange(4), jnp.arange(4), jnp.arange(16), indexing="ij"
    )
    masks = jnp.array([MASKS_A, MASKS_B])
    y_mask, z_mask = masks[half, y_at], masks[half, z_at]
    piece = col ^ (y_mask + 4 * z_mask)
    return (piece * 32 + half * 16 + low).reshape(-1).astype(jnp.int32)


def per_device(residual, interaction, commands, slope_valid, frame_valid):
    block_rows = interaction.shape[0]
    row, col = lax.axis_index("row"), lax.axis_index("col")
    order = frame_order(col)
    pick = (jnp.arange(FRAMES, dtype=jnp.int32)[None, :] == order[:, None]).astype(jnp.bfloat16)
    ordered = lax.dot_general(
        pick, commands, (((1,), (1,)), ((), ())), preferred_element_type=jnp.float32
    ).astype(jnp.bfloat16)
    product = lax.dot_general(
        ordered, interaction, (((1,), (1,)), ((), ())), preferred_element_type=jnp.float32
    ).astype(jnp.bfloat16)
    kept_a, sent_a, kept_b, sent_b = jnp.split(product, 4, axis=0)
    for swap, first, second in ((y_swap, 1, 3), (z_swap, 1, 3)):
        got_a = lax.ppermute(sent_a, "col", swap(first))
        got_b = lax.ppermute(sent_b, "col", swap(second))
        kept_a, kept_b = add(kept_a, got_a), add(kept_b, got_b)
        kept_a, sent_a = jnp.split(kept_a, 2, axis=0)
        kept_b, sent_b = jnp.split(kept_b, 2, axis=0)
        got_a = lax.ppermute(sent_a, "col", swap(second))
        got_b = lax.ppermute(sent_b, "col", swap(first))
        if swap is y_swap:
            kept_a, kept_b = add(kept_a, got_a), add(kept_b, got_b)
            kept_a, sent_a = jnp.split(kept_a, 2, axis=0)
            kept_b, sent_b = jnp.split(kept_b, 2, axis=0)
    summed = jnp.concatenate([kept_a, kept_b]).astype(jnp.float32) + jnp.concatenate(
        [got_a, got_b]
    ).astype(jnp.float32)
    row_mask = jnp.broadcast_to(slope_valid[:, None], (15, SBLK)).reshape(-1).astype(jnp.float32)
    slopes = (
        (residual.T.astype(jnp.float32) + summed)
        * row_mask[None, :]
        * frame_valid[:, None].astype(jnp.float32)
    ).astype(jnp.bfloat16)

    flip = [(r * 16 + c, c * 16 + r) for r in range(16) for c in range(16)]
    other = lax.ppermute(slopes, ("row", "col"), flip)
    mine = ring_gather(slopes, "col", z_turn)
    other = jnp.concatenate([other, lax.ppermute(other, "row", [(r, r ^ 8) for r in range(16)])])
    other = ring_gather(other, "row", x_turn)
    mine = ring_gather(mine, "col", y_turn)
    other = jnp.concatenate([other, lax.ppermute(other, "row", [(r, r ^ 1) for r in range(16)])])

    def turned(frames, step):
        half = frames.shape[0] // 2
        far = step(frames, 2)
        return jnp.concatenate([frames, step(frames, -1), step(frames, 1), far[:half], far[half:]])

    base = jnp.arange(32)
    def step_of(shift, width):
        low = (1 << shift) * 32
        def step(frames, by):
            digit = (frames // low) % width
            return frames + (((digit + by) % width) - digit) * low
        return step

    mine_at = turned(turned(base + col * 32, step_of(2, 4)), step_of(0, 4))
    other_at = base + row * 32
    other_at = jnp.concatenate([other_at, step_of(3, 2)(other_at, 1)])
    other_at = turned(other_at, step_of(1, 4))
    other_at = jnp.concatenate([other_at, step_of(0, 2)(other_at, 1)])
    match = (mine_at[:, None] == other_at[None, :]).astype(jnp.bfloat16)
    other = lax.dot_general(
        match, other, (((1,), (0,)), ((), ())), preferred_element_type=jnp.float32
    ).astype(jnp.bfloat16)
    row_ids = row * block_rows + jnp.arange(block_rows, dtype=jnp.int32)[:, None]
    col_ids = col * block_rows + jnp.arange(block_rows, dtype=jnp.int32)[None, :]
    tile = (
        lax.dot_general(mine, other, (((0,), (0,)), ((), ())), preferred_element_type=jnp.float32)
        / FRAMES
    )
    return jnp.where(row_ids <= col_ids, tile, jnp.float32(0.0)).astype(jnp.bfloat16)


def solution(mesh):
    placed = (P("row", "col"), P("row", "col"), P("col", None), P("row"), P("col"))
    return jax.shard_map(
        per_device, mesh=mesh, in_specs=placed, out_specs=P("row", "col"), check_vma=False
    )
```

```python
import functools

import jax
import jax.numpy as jnp
from jax import lax
from jax.experimental import pallas as pl
from jax.experimental.pallas import tpu as pltpu
from jax.sharding import PartitionSpec as P

SBLK = 128
FRAMES = 512
BF16 = jnp.bfloat16
F32 = jnp.float32
WHOLE = pl.BlockSpec(memory_space=pltpu.VMEM)
SCALAR = pl.BlockSpec(memory_space=pltpu.SMEM)


def y_swap(mask):
    return [(c, c ^ mask) for c in range(16)]


def z_swap(mask):
    return [(c, c ^ (4 * mask)) for c in range(16)]


def y_turn(by):
    return [(c, (c & 12) | ((c + by) & 3)) for c in range(16)]


def z_turn(by):
    return [(c, (c + 4 * by) & 15) for c in range(16)]


def x_turn(by):
    return [(r, (r & 9) | ((r + 2 * by) & 6)) for r in range(16)]


def flip_pairs():
    pairs = []
    for r in range(16):
        for c in range(16):
            z_hi, y = c >> 2, c & 3
            x = (((r >> 1) & 3) + y) & 3
            to = (z_hi >> 1) * 8 + x * 2 + (z_hi & 1)
            pairs.append((r * 16 + c, to * 16 + r))
    return pairs


def add(one, other):
    return (one.astype(F32) + other.astype(F32)).astype(BF16)


def shape(rows, cols):
    return jax.ShapeDtypeStruct((rows, cols), BF16)


def first_kernel(at_ref, commands_ref, interaction_ref, sent_a, sent_b, ordered_ref):
    col = at_ref[1]
    out = lax.broadcasted_iota(jnp.int32, (FRAMES, FRAMES), 0)
    src = lax.broadcasted_iota(jnp.int32, (FRAMES, FRAMES), 1)
    half = out >> 8
    low = out & 15

    def mask_of(at):
        one, two = at & 1, at >> 1
        return jnp.where(half == 0, (one << 1) | (one ^ two), at ^ two)

    piece = col ^ (mask_of((out >> 6) & 3) + 4 * mask_of((out >> 4) & 3))
    pick = (src == piece * 32 + half * 16 + low).astype(F32).astype(BF16)
    ordered = lax.dot_general(
        pick, commands_ref[...], (((1,), (1,)), ((), ())), preferred_element_type=F32
    ).astype(BF16)
    sent_a[...] = jnp.dot(
        ordered[128:256], interaction_ref[...], preferred_element_type=F32
    ).astype(BF16)
    sent_b[...] = jnp.dot(
        ordered[384:512], interaction_ref[...], preferred_element_type=F32
    ).astype(BF16)
    ordered_ref[:128] = ordered[:128]
    ordered_ref[128:] = ordered[256:384]


def second_kernel(ordered_ref, interaction_ref, kept_a, kept_b):
    kept_a[...] = jnp.dot(
        ordered_ref[:128], interaction_ref[...], preferred_element_type=F32
    ).astype(BF16)
    kept_b[...] = jnp.dot(
        ordered_ref[128:], interaction_ref[...], preferred_element_type=F32
    ).astype(BF16)


def halves_kernel(left, right, flipped, low, high, same):
    half = low.shape[0]
    low[...] = left[:half]
    high[...] = right[half:]
    same[...] = flipped[...]


def join_kernel(at_ref, own, left, right, far_a, far_b, flipped, pair, mine, near):
    z = at_ref[1] >> 2

    def put(by, start, ref):
        first = pl.multiple_of(((z + by) & 3) * 32 + start, 16)
        mine[pl.ds(first, ref.shape[0])] = ref[...]

    put(0, 0, own)
    put(3, 0, left)
    put(1, 0, right)
    put(2, 0, far_a)
    put(2, 16, far_b)
    z_lo = at_ref[0] >> 3
    near[pl.ds(pl.multiple_of(z_lo * 32, 32), 32)] = flipped[...]
    near[pl.ds(pl.multiple_of((1 - z_lo) * 32, 32), 32)] = pair[...]


def split_kernel(y_left, y_right, near, x_left, x_right, y_low, y_high, x_low, x_high, joined):
    y_low[...] = y_left[:64]
    y_high[...] = y_right[64:]
    x_low[...] = x_left[:32]
    x_high[...] = x_right[32:]
    joined[:64] = near[...]
    joined[64:128] = x_left[...]
    joined[128:] = x_right[...]


def stack_kernel(one, two, out):
    half = one.shape[0]
    out[:half] = one[...]
    out[half:] = two[...]


def turn_kernel(own, left, right, out):
    for at, ref in enumerate((own, left, right)):
        out[:, at * 128 : at * 128 + 128] = ref[...].T


def last_kernel(
    at_ref, early, far_a, far_b, near, near_far, other, other_far, out, lhs, rhs
):
    row, col = at_ref[0], at_ref[1]
    rows, columns = out.shape

    @pl.when(row <= col)
    def _():
        @pl.when(pl.program_id(0) == 0)
        def _():
            y = col & 3
            for at, by in enumerate((0, 3, 1)):
                lane = pl.multiple_of(((y + by) & 3) * 128, 128)
                lhs[:, pl.ds(lane, 128)] = early[:, at * 128 : at * 128 + 128]
            lane = pl.multiple_of(((y + 2) & 3) * 128, 128)
            far = jnp.concatenate([far_a[...], far_b[...]], axis=0)
            lhs[:, pl.ds(lane, 128)] = far.T
            x, core = (row >> 1) & 3, row & 1
            for swap, most, rest in ((0, near, near_far), (1, other, other_far)):
                for at, by in enumerate((0, 3, 1, 2)):
                    ref, at = (most, at) if at < 3 else (rest, 0)
                    y_from = (x + by - (col >> 1)) & 3
                    for z_lo in range(2):
                        z_from = z_lo * 2 + (core ^ swap)
                        first = pl.multiple_of(y_from * 128 + z_from * 32, 32)
                        rhs[pl.ds(first, 32)] = ref[at * 64 + z_lo * 32 : at * 64 + z_lo * 32 + 32]

        start = pl.multiple_of(pl.program_id(0) * rows, rows)
        tile = jnp.dot(lhs[pl.ds(start, rows)], rhs[...], preferred_element_type=F32) * (
            1.0 / FRAMES
        )

        @pl.when(row < col)
        def _():
            out[...] = tile.astype(BF16)

        @pl.when(row == col)
        def _():
            down = lax.broadcasted_iota(jnp.int32, tile.shape, 0) + start
            across = lax.broadcasted_iota(jnp.int32, tile.shape, 1)
            out[...] = jnp.where(down <= across, tile, 0.0).astype(BF16)

    @pl.when(row > col)
    def _():
        out[...] = jnp.zeros_like(out)


def per_device(residual, interaction, commands, slope_valid, frame_valid):
    rows, width = interaction.shape
    row, col = lax.axis_index("row"), lax.axis_index("col")
    at = jnp.stack([row, col]).astype(jnp.int32)
    limit = pltpu.CompilerParams(vmem_limit_bytes=48 * 1024 * 1024)
    call = functools.partial(pl.pallas_call, compiler_params=limit)
    turned = interaction.T
    sent_a, sent_b, ordered = call(
        first_kernel,
        out_shape=(shape(128, rows), shape(128, rows), shape(256, width)),
        in_specs=[SCALAR, WHOLE, WHOLE],
        out_specs=(WHOLE, WHOLE, WHOLE),
        cost_estimate=pl.CostEstimate(
            flops=2 * 256 * width * rows, bytes_accessed=1600000, transcendentals=0
        ),
    )(at, commands, turned)
    got_a = lax.ppermute(sent_a, "col", y_swap(1))
    got_b = lax.ppermute(sent_b, "col", y_swap(3))
    kept_a, kept_b = call(
        second_kernel,
        out_shape=(shape(128, rows), shape(128, rows)),
        in_specs=[WHOLE, WHOLE],
        out_specs=(WHOLE, WHOLE),
        cost_estimate=pl.CostEstimate(
            flops=2 * 256 * width * rows, bytes_accessed=1600000, transcendentals=0
        ),
    )(ordered, turned)
    for swap_a, swap_b in (
        (y_swap(3), y_swap(1)),
        (z_swap(1), z_swap(3)),
        (z_swap(3), z_swap(1)),
    ):
        half = kept_a.shape[0] // 2
        sent_a, sent_b = add(kept_a[half:], got_a[half:]), add(kept_b[half:], got_b[half:])
        next_a = lax.ppermute(sent_a, "col", swap_a)
        next_b = lax.ppermute(sent_b, "col", swap_b)
        kept_a, kept_b = add(kept_a[:half], got_a[:half]), add(kept_b[:half], got_b[:half])
        got_a, got_b = next_a, next_b
    summed = jnp.concatenate([kept_a, kept_b]).astype(F32) + jnp.concatenate(
        [got_a, got_b]
    ).astype(F32)
    row_mask = jnp.broadcast_to(slope_valid[:, None], (rows // SBLK, SBLK)).reshape(-1)
    slopes = (
        (residual.T.astype(F32) + summed)
        * row_mask[None, :].astype(F32)
        * frame_valid[:, None].astype(F32)
    ).astype(BF16)

    left = lax.ppermute(slopes, "col", z_turn(1))
    right = lax.ppermute(slopes, "col", z_turn(-1))
    flipped = lax.ppermute(slopes, ("row", "col"), flip_pairs())
    low, high, flipped = call(
        halves_kernel,
        out_shape=(shape(16, rows), shape(16, rows), shape(32, rows)),
        in_specs=[WHOLE] * 3,
        out_specs=(WHOLE,) * 3,
    )(left, right, flipped)
    far_a = lax.ppermute(low, "col", z_turn(1))
    far_b = lax.ppermute(high, "col", z_turn(-1))
    pair = lax.ppermute(flipped, "row", [(r, r ^ 8) for r in range(16)])
    mine, near = call(
        join_kernel,
        out_shape=(shape(128, rows), shape(64, rows)),
        in_specs=[SCALAR] + [WHOLE] * 7,
        out_specs=(WHOLE,) * 2,
    )(at, slopes, left, right, far_a, far_b, flipped, pair)
    left = lax.ppermute(mine, "col", y_turn(1))
    right = lax.ppermute(mine, "col", y_turn(-1))
    x_left = lax.ppermute(near, "row", x_turn(1))
    x_right = lax.ppermute(near, "row", x_turn(-1))
    low, high, x_low, x_high, near = call(
        split_kernel,
        out_shape=(shape(64, rows),) * 2 + (shape(32, rows),) * 2 + (shape(192, rows),),
        in_specs=[WHOLE] * 5,
        out_specs=(WHOLE,) * 5,
    )(left, right, near, x_left, x_right)
    far_a = lax.ppermute(low, "col", y_turn(1))
    far_b = lax.ppermute(high, "col", y_turn(-1))
    x_far_a = lax.ppermute(x_low, "row", x_turn(1))
    x_far_b = lax.ppermute(x_high, "row", x_turn(-1))
    cores = [(r, r ^ 1) for r in range(16)]
    other = lax.ppermute(near, "row", cores)
    near_far = call(
        stack_kernel, out_shape=shape(64, rows), in_specs=[WHOLE] * 2, out_specs=WHOLE
    )(x_far_a, x_far_b)
    other_far = lax.ppermute(near_far, "row", cores)
    early = call(
        turn_kernel,
        out_shape=shape(rows, 384),
        in_specs=[WHOLE] * 3,
        out_specs=WHOLE,
    )(mine, left, right)
    steps = 5
    return call(
        last_kernel,
        grid=(steps,),
        out_shape=shape(rows, rows),
        in_specs=[SCALAR] + [WHOLE] * 7,
        out_specs=pl.BlockSpec((rows // steps, rows), lambda i: (i, 0)),
        scratch_shapes=[pltpu.VMEM((rows, FRAMES), BF16), pltpu.VMEM((FRAMES, rows), BF16)],
        cost_estimate=pl.CostEstimate(
            flops=2 * FRAMES * rows * rows, bytes_accessed=2 * rows * rows, transcendentals=0
        ),
    )(at, early, far_a, far_b, near, near_far, other, other_far)


def solution(mesh):
    placed = (P("row", "col"), P("row", "col"), P("col", None), P("row"), P("col"))
    return jax.shard_map(
        per_device, mesh=mesh, in_specs=placed, out_specs=P("row", "col"), check_vma=False
    )
```

```python
import functools

import jax
import jax.numpy as jnp
from jax import lax
from jax.experimental import pallas as pl
from jax.experimental.pallas import tpu as pltpu
from jax.sharding import PartitionSpec as P

SBLK = 128
FRAMES = 512
BF16 = jnp.bfloat16
F32 = jnp.float32
WHOLE = pl.BlockSpec(memory_space=pltpu.VMEM)
SCALAR = pl.BlockSpec(memory_space=pltpu.SMEM)


def y_swap(mask):
    return [(c, c ^ mask) for c in range(16)]


def z_swap(mask):
    return [(c, c ^ (4 * mask)) for c in range(16)]


def y_turn(by):
    return [(c, (c & 12) | ((c + by) & 3)) for c in range(16)]


def z_turn(by):
    return [(c, (c + 4 * by) & 15) for c in range(16)]


def x_turn(by):
    return [(r, (r & 9) | ((r + 2 * by) & 6)) for r in range(16)]


def flip_pairs():
    pairs = []
    for r in range(16):
        for c in range(16):
            z_hi, y = c >> 2, c & 3
            x = (((r >> 1) & 3) + y) & 3
            to = (z_hi >> 1) * 8 + x * 2 + (z_hi & 1)
            pairs.append((r * 16 + c, to * 16 + r))
    return pairs


def add(one, other):
    return (one.astype(F32) + other.astype(F32)).astype(BF16)


def shape(rows, cols):
    return jax.ShapeDtypeStruct((rows, cols), BF16)


def first_kernel(at_ref, commands_ref, interaction_ref, sent_a, sent_b, ordered_ref):
    col = at_ref[1]
    out = lax.broadcasted_iota(jnp.int32, (FRAMES, FRAMES), 0)
    src = lax.broadcasted_iota(jnp.int32, (FRAMES, FRAMES), 1)
    half = out >> 8
    low = out & 15

    def mask_of(at):
        one, two = at & 1, at >> 1
        return jnp.where(half == 0, (one << 1) | (one ^ two), at ^ two)

    piece = ((out >> 4) & 3) * 4 + ((col & 3) ^ mask_of((out >> 6) & 3))
    pick = (src == piece * 32 + half * 16 + low).astype(F32).astype(BF16)
    ordered = lax.dot_general(
        pick, commands_ref[...], (((1,), (1,)), ((), ())), preferred_element_type=F32
    ).astype(BF16)
    sent_a[...] = jnp.dot(
        ordered[128:256], interaction_ref[...], preferred_element_type=F32
    ).astype(BF16)
    sent_b[...] = jnp.dot(
        ordered[384:512], interaction_ref[...], preferred_element_type=F32
    ).astype(BF16)
    ordered_ref[:128] = ordered[:128]
    ordered_ref[128:] = ordered[256:384]


def second_kernel(ordered_ref, interaction_ref, kept_a, kept_b):
    kept_a[...] = jnp.dot(
        ordered_ref[:128], interaction_ref[...], preferred_element_type=F32
    ).astype(BF16)
    kept_b[...] = jnp.dot(
        ordered_ref[128:], interaction_ref[...], preferred_element_type=F32
    ).astype(BF16)


def third_kernel(at_ref, kept_a, got_a, kept_b, got_b, residual, out_a, out_b):
    own = pl.ds(pl.multiple_of((at_ref[1] >> 2) * 16, 16), 16)
    for at, (kept, got, out) in enumerate(((kept_a, got_a, out_a), (kept_b, got_b, out_b))):
        out[...] = (kept[...].astype(F32) + got[...].astype(F32)).astype(BF16)
        extra = residual[at * 16 : at * 16 + 16].astype(F32)
        out[own] = (kept[own].astype(F32) + got[own].astype(F32) + extra).astype(BF16)


def slopes_kernel(
    at_ref, kept_a, got_a, kept_b, got_b, row_mask, own, left, right, far, mine, turned
):
    z = at_ref[1] >> 2
    across = row_mask[...]
    for at, (kept, got) in enumerate(((kept_a, got_a), (kept_b, got_b))):
        for by, frames in ((0, own), (3, left), (1, right), (2, far)):
            first = pl.multiple_of(((z + by) & 3) * 16, 16)
            part = pl.ds(first, 16)
            total = kept[part].astype(F32) + got[part].astype(F32)
            keep = frames[at * 16 : at * 16 + 16, :1]
            mine[pl.ds(pl.multiple_of(first + at * 64, 16), 16)] = (total * across * keep).astype(
                BF16
            )
    turned[...] = mine[pl.ds(pl.multiple_of((z & 1) * 64, 64), 64)]


def halves_kernel(left, right, low, high):
    half = low.shape[0]
    low[...] = left[:half]
    high[...] = right[half:]


def split_kernel(near, x_left, x_right, x_low, x_high, joined):
    x_low[...] = x_left[:32]
    x_high[...] = x_right[32:]
    joined[:64] = near[...]
    joined[64:128] = x_left[...]
    joined[128:] = x_right[...]


def stack_kernel(one, two, out):
    half = one.shape[0]
    out[:half] = one[...]
    out[half:] = two[...]


def turn_kernel(own, left, right, out):
    for at, ref in enumerate((own, left, right)):
        out[:, at * 128 : at * 128 + 128] = ref[...].T


def last_kernel(
    at_ref, early, far_a, far_b, near, near_far, other, other_far, out, lhs, rhs
):
    row, col = at_ref[0], at_ref[1]
    rows, columns = out.shape

    @pl.when(row <= col)
    def _():
        @pl.when(pl.program_id(0) == 0)
        def _():
            y = col & 3
            for at, by in enumerate((0, 3, 1)):
                lane = pl.multiple_of(((y + by) & 3) * 128, 128)
                lhs[:, pl.ds(lane, 128)] = early[:, at * 128 : at * 128 + 128]
            lane = pl.multiple_of(((y + 2) & 3) * 128, 128)
            far = jnp.concatenate([far_a[...], far_b[...]], axis=0)
            lhs[:, pl.ds(lane, 128)] = far.T
            x, core = (row >> 1) & 3, row & 1
            for half, most, rest in ((core, near, near_far), (1 - core, other, other_far)):
                for at, by in enumerate((0, 3, 1, 2)):
                    ref, at = (most, at) if at < 3 else (rest, 0)
                    y_from = (x + by - (col >> 1)) & 3
                    first = pl.multiple_of(y_from * 128 + half * 64, 64)
                    rhs[pl.ds(first, 64)] = ref[at * 64 : at * 64 + 64]

        start = pl.multiple_of(pl.program_id(0) * rows, rows)
        for first in range(0, columns, 640):
            span = slice(first, first + 640)

            @pl.when(jnp.logical_or(row < col, start < first + 640))
            def _():
                tile = jnp.dot(
                    lhs[pl.ds(start, rows)], rhs[:, span], preferred_element_type=F32
                ) * (1.0 / FRAMES)
                whole = jnp.logical_or(row < col, start + rows <= first)

                @pl.when(whole)
                def _():
                    out[:, span] = tile.astype(BF16)

                @pl.when(jnp.logical_not(whole))
                def _():
                    down = lax.broadcasted_iota(jnp.int32, tile.shape, 0) + start
                    across = lax.broadcasted_iota(jnp.int32, tile.shape, 1) + first
                    out[:, span] = jnp.where(down <= across, tile, 0.0).astype(BF16)

            @pl.when(jnp.logical_not(jnp.logical_or(row < col, start < first + 640)))
            def _():
                out[:, span] = jnp.zeros((rows, 640), BF16)

    @pl.when(row > col)
    def _():
        out[...] = jnp.zeros_like(out)


def per_device(residual, interaction, commands, slope_valid, frame_valid):
    rows, width = interaction.shape
    row, col = lax.axis_index("row"), lax.axis_index("col")
    at = jnp.stack([row, col]).astype(jnp.int32)
    limit = pltpu.CompilerParams(vmem_limit_bytes=48 * 1024 * 1024)
    call = functools.partial(pl.pallas_call, compiler_params=limit)
    turned = interaction.T
    sent_a, sent_b, ordered = call(
        first_kernel,
        out_shape=(shape(128, rows), shape(128, rows), shape(256, width)),
        in_specs=[SCALAR, WHOLE, WHOLE],
        out_specs=(WHOLE, WHOLE, WHOLE),
        cost_estimate=pl.CostEstimate(
            flops=2 * 256 * width * rows, bytes_accessed=1600000, transcendentals=0
        ),
    )(at, commands, turned)
    got_a = lax.ppermute(sent_a, "col", y_swap(1))
    got_b = lax.ppermute(sent_b, "col", y_swap(3))
    kept_a, kept_b = call(
        second_kernel,
        out_shape=(shape(128, rows), shape(128, rows)),
        in_specs=[WHOLE, WHOLE],
        out_specs=(WHOLE, WHOLE),
        cost_estimate=pl.CostEstimate(
            flops=2 * 256 * width * rows, bytes_accessed=1600000, transcendentals=0
        ),
    )(ordered, turned)
    frames = jnp.broadcast_to(frame_valid[:, None], (32, 128)).astype(F32)
    frames_left = lax.ppermute(frames, "col", z_turn(1))
    frames_right = lax.ppermute(frames, "col", z_turn(-1))
    frames_far = lax.ppermute(frames, "col", z_turn(2))
    sent_a, sent_b = add(kept_a[64:], got_a[64:]), add(kept_b[64:], got_b[64:])
    next_a = lax.ppermute(sent_a, "col", y_swap(3))
    next_b = lax.ppermute(sent_b, "col", y_swap(1))
    kept_a, kept_b = add(kept_a[:64], got_a[:64]), add(kept_b[:64], got_b[:64])
    kept_a, kept_b = call(
        third_kernel,
        out_shape=(shape(64, rows),) * 2,
        in_specs=[SCALAR] + [WHOLE] * 5,
        out_specs=(WHOLE,) * 2,
    )(at, kept_a, next_a, kept_b, next_b, residual.T)
    got_a = lax.ppermute(kept_a, "col", z_swap(1))
    got_b = lax.ppermute(kept_b, "col", z_swap(3))
    kept_a, kept_b = add(kept_a, got_a), add(kept_b, got_b)
    got_a = lax.ppermute(kept_a, "col", z_swap(3))
    got_b = lax.ppermute(kept_b, "col", z_swap(1))
    row_mask = jnp.broadcast_to(slope_valid[:, None], (rows // SBLK, SBLK)).reshape(1, rows)
    mine, near = call(
        slopes_kernel,
        out_shape=(shape(128, rows), shape(64, rows)),
        in_specs=[SCALAR] + [WHOLE] * 9,
        out_specs=(WHOLE,) * 2,
    )(
        at,
        kept_a,
        got_a,
        kept_b,
        got_b,
        row_mask.astype(F32),
        frames,
        frames_left,
        frames_right,
        frames_far,
    )

    left = lax.ppermute(mine, "col", y_turn(1))
    right = lax.ppermute(mine, "col", y_turn(-1))
    near = lax.ppermute(near, ("row", "col"), flip_pairs())
    x_left = lax.ppermute(near, "row", x_turn(1))
    x_right = lax.ppermute(near, "row", x_turn(-1))
    low, high = call(
        halves_kernel,
        out_shape=(shape(64, rows),) * 2,
        in_specs=[WHOLE] * 2,
        out_specs=(WHOLE,) * 2,
        cost_estimate=pl.CostEstimate(flops=30000000000, bytes_accessed=983040, transcendentals=0),
    )(left, right)
    far_a = lax.ppermute(low, "col", y_turn(1))
    far_b = lax.ppermute(high, "col", y_turn(-1))
    x_low, x_high, near = call(
        split_kernel,
        out_shape=(shape(32, rows),) * 2 + (shape(192, rows),),
        in_specs=[WHOLE] * 3,
        out_specs=(WHOLE,) * 3,
    )(near, x_left, x_right)
    x_far_a = lax.ppermute(x_low, "row", x_turn(1))
    x_far_b = lax.ppermute(x_high, "row", x_turn(-1))
    cores = [(r, r ^ 1) for r in range(16)]
    other = lax.ppermute(near, "row", cores)
    near_far = call(
        stack_kernel, out_shape=shape(64, rows), in_specs=[WHOLE] * 2, out_specs=WHOLE
    )(x_far_a, x_far_b)
    other_far = lax.ppermute(near_far, "row", cores)
    early = call(
        turn_kernel,
        out_shape=shape(rows, 384),
        in_specs=[WHOLE] * 3,
        out_specs=WHOLE,
    )(mine, left, right)
    steps = 10
    return call(
        last_kernel,
        grid=(steps,),
        out_shape=shape(rows, rows),
        in_specs=[SCALAR] + [WHOLE] * 7,
        out_specs=pl.BlockSpec((rows // steps, rows), lambda i: (i, 0)),
        scratch_shapes=[pltpu.VMEM((rows, FRAMES), BF16), pltpu.VMEM((FRAMES, rows), BF16)],
        cost_estimate=pl.CostEstimate(
            flops=2 * FRAMES * rows * rows, bytes_accessed=2 * rows * rows, transcendentals=0
        ),
    )(at, early, far_a, far_b, near, near_far, other, other_far)


def solution(mesh):
    placed = (P("row", "col"), P("row", "col"), P("col", None), P("row"), P("col"))
    return jax.shard_map(
        per_device, mesh=mesh, in_specs=placed, out_specs=P("row", "col"), check_vma=False
    )
```

```python
import functools

import jax
import jax.numpy as jnp
from jax import lax
from jax.experimental import pallas as pl
from jax.experimental.pallas import tpu as pltpu
from jax.sharding import PartitionSpec as P

SBLK = 128
FRAMES = 512
BF16 = jnp.bfloat16
F32 = jnp.float32
WHOLE = pl.BlockSpec(memory_space=pltpu.VMEM)
SCALAR = pl.BlockSpec(memory_space=pltpu.SMEM)


def y_swap(mask):
    return [(c, c ^ mask) for c in range(16)]


def z_swap(mask):
    return [(c, c ^ (4 * mask)) for c in range(16)]


def y_turn(by):
    return [(c, (c & 12) | ((c + by) & 3)) for c in range(16)]


def z_turn(by):
    return [(c, (c + 4 * by) & 15) for c in range(16)]


def x_turn(by):
    return [(r, (r & 9) | ((r + 2 * by) & 6)) for r in range(16)]


def flip_pairs():
    pairs = []
    for r in range(16):
        for c in range(16):
            z_hi, y = c >> 2, c & 3
            x = (((r >> 1) & 3) + y) & 3
            to = (z_hi >> 1) * 8 + x * 2 + (z_hi & 1)
            pairs.append((r * 16 + c, to * 16 + r))
    return pairs


def add(one, other):
    return (one.astype(F32) + other.astype(F32)).astype(BF16)


def shape(rows, cols):
    return jax.ShapeDtypeStruct((rows, cols), BF16)


def first_kernel(at_ref, commands_ref, interaction_ref, sent_a, sent_b, ordered_ref):
    col = at_ref[1]
    out = lax.broadcasted_iota(jnp.int32, (FRAMES, FRAMES), 0)
    src = lax.broadcasted_iota(jnp.int32, (FRAMES, FRAMES), 1)
    half = out >> 8
    low = out & 15

    def mask_of(at):
        one, two = at & 1, at >> 1
        return jnp.where(half == 0, (one << 1) | (one ^ two), at ^ two)

    piece = col ^ (mask_of((out >> 6) & 3) + 4 * mask_of((out >> 4) & 3))
    pick = (src == piece * 32 + half * 16 + low).astype(F32).astype(BF16)
    ordered = lax.dot_general(
        pick, commands_ref[...], (((1,), (1,)), ((), ())), preferred_element_type=F32
    ).astype(BF16)
    sent_a[...] = jnp.dot(
        ordered[128:256], interaction_ref[...], preferred_element_type=F32
    ).astype(BF16)
    sent_b[...] = jnp.dot(
        ordered[384:512], interaction_ref[...], preferred_element_type=F32
    ).astype(BF16)
    ordered_ref[:128] = ordered[:128]
    ordered_ref[128:] = ordered[256:384]


def second_kernel(ordered_ref, interaction_ref, kept_a, kept_b):
    kept_a[...] = jnp.dot(
        ordered_ref[:128], interaction_ref[...], preferred_element_type=F32
    ).astype(BF16)
    kept_b[...] = jnp.dot(
        ordered_ref[128:], interaction_ref[...], preferred_element_type=F32
    ).astype(BF16)


def halves_kernel(left, right, low, high):
    half = low.shape[0]
    low[...] = left[:half]
    high[...] = right[half:]


def z_join_kernel(at_ref, own, left, right, far_a, far_b, mine):
    z = at_ref[1] >> 2

    def put(by, start, ref):
        first = pl.multiple_of(((z + by) & 3) * 32 + start, 16)
        mine[pl.ds(first, ref.shape[0])] = ref[...]

    put(0, 0, own)
    put(3, 0, left)
    put(1, 0, right)
    put(2, 0, far_a)
    put(2, 16, far_b)


def pair_join_kernel(at_ref, flipped, pair, near):
    z_lo = at_ref[0] >> 3
    near[pl.ds(pl.multiple_of(z_lo * 32, 32), 32)] = flipped[...]
    near[pl.ds(pl.multiple_of((1 - z_lo) * 32, 32), 32)] = pair[...]


def split_kernel(near, x_left, x_right, x_low, x_high, joined):
    x_low[...] = x_left[:32]
    x_high[...] = x_right[32:]
    joined[:64] = near[...]
    joined[64:128] = x_left[...]
    joined[128:] = x_right[...]


def stack_kernel(one, two, after, out):
    half = one.shape[0]
    out[:half] = one[...]
    out[half:] = two[...]


BLOCKS = ((0, 480), (480, 960), (960, 1440), (1440, 1760), (1760, 1920))


def last_kernel(
    at_ref,
    own,
    left,
    right,
    far_a,
    far_b,
    near,
    near_far,
    other,
    other_far,
    out,
    lhs,
    rhs,
    held,
    done,
):
    row, col = at_ref[0], at_ref[1]
    columns = held.shape[1]
    dims = (((0,), (0,)), ((), ()))

    def sent(at, source=None):
        first, end = BLOCKS[at]
        source = held.at[first:end] if source is None else source
        return pltpu.make_async_copy(source, out.at[first:end], done.at[at])

    @pl.when(row <= col)
    def _():
        y = col & 3

        def put(by, start, ref):
            first = pl.multiple_of(((y + by) & 3) * 128 + start, 64)
            lhs[pl.ds(first, ref.shape[0])] = ref[...]

        put(0, 0, own)
        put(3, 0, left)
        put(1, 0, right)
        put(2, 0, far_a)
        put(2, 64, far_b)
        x, core = (row >> 1) & 3, row & 1
        for swap, most, rest in ((0, near, near_far), (1, other, other_far)):
            for at, by in enumerate((0, 3, 1, 2)):
                ref, at = (most, at) if at < 3 else (rest, 0)
                y_from = (x + by - (col >> 1)) & 3
                for z_lo in range(2):
                    z_from = z_lo * 2 + (core ^ swap)
                    first = pl.multiple_of(y_from * 128 + z_from * 32, 32)
                    rhs[pl.ds(first, 32)] = ref[at * 64 + z_lo * 32 : at * 64 + z_lo * 32 + 32]

    @pl.when(row < col)
    def _():
        for at, (first, end) in enumerate(BLOCKS):
            tile = lax.dot_general(lhs[:, first:end], rhs[...], dims, preferred_element_type=F32)
            held[first:end] = (tile * (1.0 / FRAMES)).astype(BF16)
            sent(at).start()

    @pl.when(row == col)
    def _():
        for at, (first, end) in enumerate(BLOCKS):
            low = first // 128 * 128
            if low:
                held[first:end, :low] = jnp.zeros((end - first, low), BF16)
            tile = lax.dot_general(
                lhs[:, first:end], rhs[:, low:], dims, preferred_element_type=F32
            ) * (1.0 / FRAMES)
            down = lax.broadcasted_iota(jnp.int32, tile.shape, 0) + first
            across = lax.broadcasted_iota(jnp.int32, tile.shape, 1) + low
            held[first:end, low:] = jnp.where(down <= across, tile, 0.0).astype(BF16)
            sent(at).start()

    @pl.when(row > col)
    def _():
        held[:480] = jnp.zeros((480, columns), BF16)
        for at, (first, end) in enumerate(BLOCKS):
            sent(at, held.at[: end - first]).start()

    for at in range(len(BLOCKS)):
        sent(at).wait()


def per_device(residual, interaction, commands, slope_valid, frame_valid):
    rows, width = interaction.shape
    row, col = lax.axis_index("row"), lax.axis_index("col")
    at = jnp.stack([row, col]).astype(jnp.int32)
    limit = pltpu.CompilerParams(vmem_limit_bytes=48 * 1024 * 1024)
    call = functools.partial(pl.pallas_call, compiler_params=limit)
    turned = interaction.T
    sent_a, sent_b, ordered = call(
        first_kernel,
        out_shape=(shape(128, rows), shape(128, rows), shape(256, width)),
        in_specs=[SCALAR, WHOLE, WHOLE],
        out_specs=(WHOLE, WHOLE, WHOLE),
        cost_estimate=pl.CostEstimate(
            flops=2 * 256 * width * rows, bytes_accessed=1600000, transcendentals=0
        ),
    )(at, commands, turned)
    got_a = lax.ppermute(sent_a, "col", y_swap(1))
    got_b = lax.ppermute(sent_b, "col", y_swap(3))
    kept_a, kept_b = call(
        second_kernel,
        out_shape=(shape(128, rows), shape(128, rows)),
        in_specs=[WHOLE, WHOLE],
        out_specs=(WHOLE, WHOLE),
        cost_estimate=pl.CostEstimate(
            flops=2 * 256 * width * rows, bytes_accessed=1600000, transcendentals=0
        ),
    )(ordered, turned)
    for swap_a, swap_b in (
        (y_swap(3), y_swap(1)),
        (z_swap(1), z_swap(3)),
        (z_swap(3), z_swap(1)),
    ):
        half = kept_a.shape[0] // 2
        sent_a, sent_b = add(kept_a[half:], got_a[half:]), add(kept_b[half:], got_b[half:])
        next_a = lax.ppermute(sent_a, "col", swap_a)
        next_b = lax.ppermute(sent_b, "col", swap_b)
        kept_a, kept_b = add(kept_a[:half], got_a[:half]), add(kept_b[:half], got_b[:half])
        got_a, got_b = next_a, next_b
    summed = jnp.concatenate([kept_a, kept_b]).astype(F32) + jnp.concatenate(
        [got_a, got_b]
    ).astype(F32)
    row_mask = jnp.broadcast_to(slope_valid[:, None], (rows // SBLK, SBLK)).reshape(-1)
    slopes = (
        (residual.T.astype(F32) + summed)
        * row_mask[None, :].astype(F32)
        * frame_valid[:, None].astype(F32)
    ).astype(BF16)

    def halves(one, two, flops):
        half = one.shape[0] // 2
        return call(
            halves_kernel,
            out_shape=(shape(half, rows),) * 2,
            in_specs=[WHOLE] * 2,
            out_specs=(WHOLE,) * 2,
            cost_estimate=pl.CostEstimate(flops=flops, bytes_accessed=983040, transcendentals=0),
        )(one, two)

    left = lax.ppermute(slopes, "col", z_turn(1))
    right = lax.ppermute(slopes, "col", z_turn(-1))
    flipped = lax.ppermute(slopes, ("row", "col"), flip_pairs())
    low, high = halves(left, right, 8000000000)
    far_a = lax.ppermute(low, "col", z_turn(1))
    far_b = lax.ppermute(high, "col", z_turn(-1))
    mine = call(
        z_join_kernel,
        out_shape=shape(128, rows),
        in_specs=[SCALAR] + [WHOLE] * 5,
        out_specs=WHOLE,
    )(at, slopes, left, right, far_a, far_b)
    left = lax.ppermute(mine, "col", y_turn(1))
    right = lax.ppermute(mine, "col", y_turn(-1))
    pair = lax.ppermute(flipped, "row", [(r, r ^ 8) for r in range(16)])
    near = call(
        pair_join_kernel,
        out_shape=shape(64, rows),
        in_specs=[SCALAR] + [WHOLE] * 2,
        out_specs=WHOLE,
    )(at, flipped, pair)
    x_left = lax.ppermute(near, "row", x_turn(1))
    x_right = lax.ppermute(near, "row", x_turn(-1))
    low, high = halves(left, right, 4000000000)
    far_a = lax.ppermute(low, "col", y_turn(1))
    far_b = lax.ppermute(high, "col", y_turn(-1))
    x_low, x_high, near = call(
        split_kernel,
        out_shape=(shape(32, rows),) * 2 + (shape(192, rows),),
        in_specs=[WHOLE] * 3,
        out_specs=(WHOLE,) * 3,
    )(near, x_left, x_right)
    x_far_a = lax.ppermute(x_low, "row", x_turn(1))
    x_far_b = lax.ppermute(x_high, "row", x_turn(-1))
    cores = [(r, r ^ 1) for r in range(16)]
    other = lax.ppermute(near, "row", cores)
    near_far = call(
        stack_kernel, out_shape=shape(64, rows), in_specs=[WHOLE] * 3, out_specs=WHOLE
    )(x_far_a, x_far_b, low)
    other_far = lax.ppermute(near_far, "row", cores)
    return call(
        last_kernel,
        out_shape=shape(rows, rows),
        in_specs=[SCALAR] + [WHOLE] * 9,
        out_specs=pl.BlockSpec(memory_space=pl.ANY),
        scratch_shapes=[
            pltpu.VMEM((FRAMES, rows), BF16),
            pltpu.VMEM((FRAMES, rows), BF16),
            pltpu.VMEM((rows, rows), BF16),
            pltpu.SemaphoreType.DMA((len(BLOCKS),)),
        ],
        cost_estimate=pl.CostEstimate(
            flops=2 * FRAMES * rows * rows, bytes_accessed=2 * rows * rows, transcendentals=0
        ),
    )(at, mine, left, right, far_a, far_b, near, near_far, other, other_far)


def solution(mesh):
    placed = (P("row", "col"), P("row", "col"), P("col", None), P("row"), P("col"))
    return jax.shard_map(
        per_device, mesh=mesh, in_specs=placed, out_specs=P("row", "col"), check_vma=False
    )
```

```python
import functools

import jax
import jax.numpy as jnp
from jax import lax
from jax.experimental import pallas as pl
from jax.experimental.pallas import tpu as pltpu
from jax.sharding import PartitionSpec as P

SBLK = 128
FRAMES = 512
BF16 = jnp.bfloat16
F32 = jnp.float32
WHOLE = pl.BlockSpec(memory_space=pltpu.VMEM)
SCALAR = pl.BlockSpec(memory_space=pltpu.SMEM)


def y_swap(mask):
    return [(c, c ^ mask) for c in range(16)]


def z_swap(mask):
    return [(c, c ^ (4 * mask)) for c in range(16)]


def y_turn(by):
    return [(c, (c & 12) | ((c + by) & 3)) for c in range(16)]


def z_turn(by):
    return [(c, (c + 4 * by) & 15) for c in range(16)]


def x_turn(by):
    return [(r, (r & 9) | ((r + 2 * by) & 6)) for r in range(16)]


def flip_pairs():
    pairs = []
    for r in range(16):
        for c in range(16):
            z_hi, y = c >> 2, c & 3
            x = (((r >> 1) & 3) + y) & 3
            to = (z_hi >> 1) * 8 + x * 2 + (z_hi & 1)
            pairs.append((r * 16 + c, to * 16 + r))
    return pairs


def add(one, other):
    return (one.astype(F32) + other.astype(F32)).astype(BF16)


def shape(rows, cols):
    return jax.ShapeDtypeStruct((rows, cols), BF16)


def first_kernel(at_ref, commands_ref, interaction_ref, sent_a, sent_b, ordered_ref):
    col = at_ref[1]
    out = lax.broadcasted_iota(jnp.int32, (FRAMES, FRAMES), 0)
    src = lax.broadcasted_iota(jnp.int32, (FRAMES, FRAMES), 1)
    half = out >> 8
    low = out & 15

    def mask_of(at):
        one, two = at & 1, at >> 1
        return jnp.where(half == 0, (one << 1) | (one ^ two), at ^ two)

    piece = col ^ (mask_of((out >> 6) & 3) + 4 * mask_of((out >> 4) & 3))
    pick = (src == piece * 32 + half * 16 + low).astype(F32).astype(BF16)
    ordered = lax.dot_general(
        pick, commands_ref[...], (((1,), (1,)), ((), ())), preferred_element_type=F32
    ).astype(BF16)
    sent_a[...] = jnp.dot(
        ordered[128:256], interaction_ref[...], preferred_element_type=F32
    ).astype(BF16)
    sent_b[...] = jnp.dot(
        ordered[384:512], interaction_ref[...], preferred_element_type=F32
    ).astype(BF16)
    ordered_ref[:128] = ordered[:128]
    ordered_ref[128:] = ordered[256:384]


def second_kernel(ordered_ref, interaction_ref, kept_a, kept_b):
    kept_a[...] = jnp.dot(
        ordered_ref[:128], interaction_ref[...], preferred_element_type=F32
    ).astype(BF16)
    kept_b[...] = jnp.dot(
        ordered_ref[128:], interaction_ref[...], preferred_element_type=F32
    ).astype(BF16)


def halves_kernel(left, right, low, high):
    half = low.shape[0]
    low[...] = left[:half]
    high[...] = right[half:]


def same_kernel(flipped, after, out):
    out[...] = flipped[...]


def join_kernel(at_ref, own, left, right, far_a, far_b, flipped, pair, mine, near):
    z = at_ref[1] >> 2

    def put(by, start, ref):
        first = pl.multiple_of(((z + by) & 3) * 32 + start, 16)
        mine[pl.ds(first, ref.shape[0])] = ref[...]

    put(0, 0, own)
    put(3, 0, left)
    put(1, 0, right)
    put(2, 0, far_a)
    put(2, 16, far_b)
    z_lo = at_ref[0] >> 3
    near[pl.ds(pl.multiple_of(z_lo * 32, 32), 32)] = flipped[...]
    near[pl.ds(pl.multiple_of((1 - z_lo) * 32, 32), 32)] = pair[...]


def gather_kernel(near, x_left, x_right, x_far_a, x_far_b, after, out):
    first = 0
    for ref in (near, x_left, x_right, x_far_a, x_far_b):
        out[first : first + ref.shape[0]] = ref[...]
        first += ref.shape[0]


def stack_kernel(one, two, out):
    half = one.shape[0]
    out[:half] = one[...]
    out[half:] = two[...]


BLOCKS = ((0, 480), (480, 960), (960, 1440), (1440, 1760), (1760, 1920))


def last_kernel(
    at_ref,
    own,
    left,
    right,
    far,
    near,
    other,
    out,
    lhs,
    rhs,
    held,
    done,
):
    row, col = at_ref[0], at_ref[1]
    columns = held.shape[1]
    dims = (((0,), (0,)), ((), ()))

    def sent(at, source=None):
        first, end = BLOCKS[at]
        source = held.at[first:end] if source is None else source
        return pltpu.make_async_copy(source, out.at[first:end], done.at[at])

    @pl.when(row <= col)
    def _():
        y = col & 3

        for by, ref in ((0, own), (3, left), (1, right), (2, far)):
            lhs[pl.ds(pl.multiple_of(((y + by) & 3) * 128, 128), 128)] = ref[...]
        x, core = (row >> 1) & 3, row & 1
        for swap, ref in ((0, near), (1, other)):
            for at, by in enumerate((0, 3, 1, 2)):
                y_from = (x + by - (col >> 1)) & 3
                for z_lo in range(2):
                    z_from = z_lo * 2 + (core ^ swap)
                    first = pl.multiple_of(y_from * 128 + z_from * 32, 32)
                    rhs[pl.ds(first, 32)] = ref[at * 64 + z_lo * 32 : at * 64 + z_lo * 32 + 32]

    @pl.when(row < col)
    def _():
        for at, (first, end) in enumerate(BLOCKS):
            tile = lax.dot_general(lhs[:, first:end], rhs[...], dims, preferred_element_type=F32)
            held[first:end] = (tile * (1.0 / FRAMES)).astype(BF16)
            sent(at).start()

    @pl.when(row == col)
    def _():
        for at, (first, end) in enumerate(BLOCKS):
            low = first // 128 * 128
            if low:
                held[first:end, :low] = jnp.zeros((end - first, low), BF16)
            tile = lax.dot_general(
                lhs[:, first:end], rhs[:, low:], dims, preferred_element_type=F32
            ) * (1.0 / FRAMES)
            down = lax.broadcasted_iota(jnp.int32, tile.shape, 0) + first
            across = lax.broadcasted_iota(jnp.int32, tile.shape, 1) + low
            held[first:end, low:] = jnp.where(down <= across, tile, 0.0).astype(BF16)
            sent(at).start()

    @pl.when(row > col)
    def _():
        held[:480] = jnp.zeros((480, columns), BF16)
        for at, (first, end) in enumerate(BLOCKS):
            sent(at, held.at[: end - first]).start()

    for at in range(len(BLOCKS)):
        sent(at).wait()


def per_device(residual, interaction, commands, slope_valid, frame_valid):
    rows, width = interaction.shape
    row, col = lax.axis_index("row"), lax.axis_index("col")
    at = jnp.stack([row, col]).astype(jnp.int32)
    limit = pltpu.CompilerParams(vmem_limit_bytes=48 * 1024 * 1024)
    call = functools.partial(pl.pallas_call, compiler_params=limit)
    turned = interaction.T
    sent_a, sent_b, ordered = call(
        first_kernel,
        out_shape=(shape(128, rows), shape(128, rows), shape(256, width)),
        in_specs=[SCALAR, WHOLE, WHOLE],
        out_specs=(WHOLE, WHOLE, WHOLE),
        cost_estimate=pl.CostEstimate(
            flops=2 * 256 * width * rows, bytes_accessed=1600000, transcendentals=0
        ),
    )(at, commands, turned)
    got_a = lax.ppermute(sent_a, "col", y_swap(1))
    got_b = lax.ppermute(sent_b, "col", y_swap(3))
    kept_a, kept_b = call(
        second_kernel,
        out_shape=(shape(128, rows), shape(128, rows)),
        in_specs=[WHOLE, WHOLE],
        out_specs=(WHOLE, WHOLE),
        cost_estimate=pl.CostEstimate(
            flops=2 * 256 * width * rows, bytes_accessed=1600000, transcendentals=0
        ),
    )(ordered, turned)
    for swap_a, swap_b in (
        (y_swap(3), y_swap(1)),
        (z_swap(1), z_swap(3)),
        (z_swap(3), z_swap(1)),
    ):
        half = kept_a.shape[0] // 2
        sent_a, sent_b = add(kept_a[half:], got_a[half:]), add(kept_b[half:], got_b[half:])
        next_a = lax.ppermute(sent_a, "col", swap_a)
        next_b = lax.ppermute(sent_b, "col", swap_b)
        kept_a, kept_b = add(kept_a[:half], got_a[:half]), add(kept_b[:half], got_b[:half])
        got_a, got_b = next_a, next_b
    summed = jnp.concatenate([kept_a, kept_b]).astype(F32) + jnp.concatenate(
        [got_a, got_b]
    ).astype(F32)
    row_mask = jnp.broadcast_to(slope_valid[:, None], (rows // SBLK, SBLK)).reshape(-1)
    slopes = (
        (residual.T.astype(F32) + summed)
        * row_mask[None, :].astype(F32)
        * frame_valid[:, None].astype(F32)
    ).astype(BF16)

    def halves(one, two, flops):
        half = one.shape[0] // 2
        return call(
            halves_kernel,
            out_shape=(shape(half, rows),) * 2,
            in_specs=[WHOLE] * 2,
            out_specs=(WHOLE,) * 2,
            cost_estimate=pl.CostEstimate(flops=flops, bytes_accessed=983040, transcendentals=0),
        )(one, two)

    left = lax.ppermute(slopes, "col", z_turn(1))
    right = lax.ppermute(slopes, "col", z_turn(-1))
    flipped = lax.ppermute(slopes, ("row", "col"), flip_pairs())
    low, high = halves(left, right, 8000000000)
    far_a = lax.ppermute(low, "col", z_turn(1))
    far_b = lax.ppermute(high, "col", z_turn(-1))
    flipped = call(
        same_kernel, out_shape=shape(32, rows), in_specs=[WHOLE] * 2, out_specs=WHOLE
    )(flipped, low)
    pair = lax.ppermute(flipped, "row", [(r, r ^ 8) for r in range(16)])
    mine, near = call(
        join_kernel,
        out_shape=(shape(128, rows), shape(64, rows)),
        in_specs=[SCALAR] + [WHOLE] * 7,
        out_specs=(WHOLE,) * 2,
    )(at, slopes, left, right, far_a, far_b, flipped, pair)
    left = lax.ppermute(mine, "col", y_turn(1))
    right = lax.ppermute(mine, "col", y_turn(-1))
    x_left = lax.ppermute(near, "row", x_turn(1))
    x_right = lax.ppermute(near, "row", x_turn(-1))
    low, high = halves(left, right, 8000000000)
    far_a = lax.ppermute(low, "col", y_turn(1))
    far_b = lax.ppermute(high, "col", y_turn(-1))
    far = call(
        stack_kernel,
        out_shape=shape(128, rows),
        in_specs=[WHOLE] * 2,
        out_specs=WHOLE,
        cost_estimate=pl.CostEstimate(flops=8000000000, bytes_accessed=983040, transcendentals=0),
    )(far_a, far_b)
    x_low, x_high = halves(x_left, x_right, 0)
    x_far_a = lax.ppermute(x_low, "row", x_turn(1))
    x_far_b = lax.ppermute(x_high, "row", x_turn(-1))
    near = call(
        gather_kernel, out_shape=shape(256, rows), in_specs=[WHOLE] * 6, out_specs=WHOLE
    )(near, x_left, x_right, x_far_a, x_far_b, low)
    other = lax.ppermute(near, "row", [(r, r ^ 1) for r in range(16)])
    return call(
        last_kernel,
        out_shape=shape(rows, rows),
        in_specs=[SCALAR] + [WHOLE] * 6,
        out_specs=pl.BlockSpec(memory_space=pl.ANY),
        scratch_shapes=[
            pltpu.VMEM((FRAMES, rows), BF16),
            pltpu.VMEM((FRAMES, rows), BF16),
            pltpu.VMEM((rows, rows), BF16),
            pltpu.SemaphoreType.DMA((len(BLOCKS),)),
        ],
        cost_estimate=pl.CostEstimate(
            flops=2 * FRAMES * rows * rows, bytes_accessed=2 * rows * rows, transcendentals=0
        ),
    )(at, mine, left, right, far, near, other)


def solution(mesh):
    placed = (P("row", "col"), P("row", "col"), P("col", None), P("row"), P("col"))
    return jax.shard_map(
        per_device, mesh=mesh, in_specs=placed, out_specs=P("row", "col"), check_vma=False
    )
```

```python
import functools

import jax
import jax.numpy as jnp
from jax import lax
from jax.experimental import pallas as pl
from jax.experimental.pallas import tpu as pltpu
from jax.sharding import PartitionSpec as P

SBLK = 128
FRAMES = 512
BF16 = jnp.bfloat16
F32 = jnp.float32
WHOLE = pl.BlockSpec(memory_space=pltpu.VMEM)
SCALAR = pl.BlockSpec(memory_space=pltpu.SMEM)


def y_swap(mask):
    return [(c, c ^ mask) for c in range(16)]


def z_swap(mask):
    return [(c, c ^ (4 * mask)) for c in range(16)]


def y_turn(by):
    return [(c, (c & 12) | ((c + by) & 3)) for c in range(16)]


def z_turn(by):
    return [(c, (c + 4 * by) & 15) for c in range(16)]


def x_turn(by):
    return [(r, (r & 9) | ((r + 2 * by) & 6)) for r in range(16)]


def flip_pairs(which):
    pairs = []
    for r in range(16):
        for c in range(16):
            z_hi, y = c >> 2, c & 3
            x = (((r >> 1) & 3) + y) & 3
            z_lo = (z_hi >> 1) ^ which
            if r >= 8 or z_lo == 0:
                pairs.append((r * 16 + c, (z_lo * 8 + x * 2 + (z_hi & 1)) * 16 + r))
    return pairs


def add(one, other):
    return (one.astype(F32) + other.astype(F32)).astype(BF16)


def shape(rows, cols):
    return jax.ShapeDtypeStruct((rows, cols), BF16)


def first_kernel(at_ref, commands_ref, interaction_ref, sent_a, sent_b, ordered_ref):
    col = at_ref[1]
    out = lax.broadcasted_iota(jnp.int32, (FRAMES, FRAMES), 0)
    src = lax.broadcasted_iota(jnp.int32, (FRAMES, FRAMES), 1)
    half = out >> 8
    low = out & 15

    def mask_of(at):
        one, two = at & 1, at >> 1
        return jnp.where(half == 0, (one << 1) | (one ^ two), at ^ two)

    piece = col ^ (mask_of((out >> 6) & 3) + 4 * mask_of((out >> 4) & 3))
    pick = (src == piece * 32 + half * 16 + low).astype(F32).astype(BF16)
    ordered = lax.dot_general(
        pick, commands_ref[...], (((1,), (1,)), ((), ())), preferred_element_type=F32
    ).astype(BF16)
    sent_a[...] = jnp.dot(
        ordered[128:256], interaction_ref[...], preferred_element_type=F32
    ).astype(BF16)
    sent_b[...] = jnp.dot(
        ordered[384:512], interaction_ref[...], preferred_element_type=F32
    ).astype(BF16)
    ordered_ref[:128] = ordered[:128]
    ordered_ref[128:] = ordered[256:384]


def second_kernel(ordered_ref, interaction_ref, kept_a, kept_b):
    kept_a[...] = jnp.dot(
        ordered_ref[:128], interaction_ref[...], preferred_element_type=F32
    ).astype(BF16)
    kept_b[...] = jnp.dot(
        ordered_ref[128:], interaction_ref[...], preferred_element_type=F32
    ).astype(BF16)


def halves_kernel(left, right, low, high):
    half = low.shape[0]
    low[...] = left[:half]
    high[...] = right[half:]


def join_kernel(at_ref, own, left, right, far_a, far_b, flipped, pair, mine, near):
    z = at_ref[1] >> 2

    def put(by, start, ref):
        first = pl.multiple_of(((z + by) & 3) * 32 + start, 16)
        mine[pl.ds(first, ref.shape[0])] = ref[...]

    put(0, 0, own)
    put(3, 0, left)
    put(1, 0, right)
    put(2, 0, far_a)
    put(2, 16, far_b)
    z_lo = at_ref[0] >> 3
    near[pl.ds(pl.multiple_of(z_lo * 32, 32), 32)] = flipped[...]
    near[pl.ds(pl.multiple_of((1 - z_lo) * 32, 32), 32)] = pair[...]


def gather_kernel(near, x_left, x_right, x_far_a, x_far_b, after, out):
    first = 0
    for ref in (near, x_left, x_right, x_far_a, x_far_b):
        out[first : first + ref.shape[0]] = ref[...]
        first += ref.shape[0]


def stack_kernel(one, two, out):
    half = one.shape[0]
    out[:half] = one[...]
    out[half:] = two[...]


BLOCKS = ((0, 480), (480, 960), (960, 1440), (1440, 1760), (1760, 1920))


def last_kernel(
    at_ref,
    own,
    left,
    right,
    far,
    near,
    other,
    out,
    lhs,
    rhs,
    held,
    done,
):
    row, col = at_ref[0], at_ref[1]
    columns = held.shape[1]
    dims = (((0,), (0,)), ((), ()))

    def sent(at, source=None):
        first, end = BLOCKS[at]
        source = held.at[first:end] if source is None else source
        return pltpu.make_async_copy(source, out.at[first:end], done.at[at])

    @pl.when(row <= col)
    def _():
        y = col & 3

        for by, ref in ((0, own), (3, left), (1, right), (2, far)):
            lhs[pl.ds(pl.multiple_of(((y + by) & 3) * 128, 128), 128)] = ref[...]
        x, core = (row >> 1) & 3, row & 1
        for swap, ref in ((0, near), (1, other)):
            for at, by in enumerate((0, 3, 1, 2)):
                y_from = (x + by - (col >> 1)) & 3
                for z_lo in range(2):
                    z_from = z_lo * 2 + (core ^ swap)
                    first = pl.multiple_of(y_from * 128 + z_from * 32, 32)
                    rhs[pl.ds(first, 32)] = ref[at * 64 + z_lo * 32 : at * 64 + z_lo * 32 + 32]

    @pl.when(row < col)
    def _():
        for at, (first, end) in enumerate(BLOCKS):
            tile = lax.dot_general(lhs[:, first:end], rhs[...], dims, preferred_element_type=F32)
            held[first:end] = (tile * (1.0 / FRAMES)).astype(BF16)
            sent(at).start()

    @pl.when(row == col)
    def _():
        for at, (first, end) in enumerate(BLOCKS):
            low = first // 128 * 128
            if low:
                held[first:end, :low] = jnp.zeros((end - first, low), BF16)
            tile = lax.dot_general(
                lhs[:, first:end], rhs[:, low:], dims, preferred_element_type=F32
            ) * (1.0 / FRAMES)
            down = lax.broadcasted_iota(jnp.int32, tile.shape, 0) + first
            across = lax.broadcasted_iota(jnp.int32, tile.shape, 1) + low
            held[first:end, low:] = jnp.where(down <= across, tile, 0.0).astype(BF16)
            sent(at).start()

    @pl.when(row > col)
    def _():
        held[:480] = jnp.zeros((480, columns), BF16)
        for at, (first, end) in enumerate(BLOCKS):
            sent(at, held.at[: end - first]).start()

    for at in range(len(BLOCKS)):
        sent(at).wait()


def per_device(residual, interaction, commands, slope_valid, frame_valid):
    rows, width = interaction.shape
    row, col = lax.axis_index("row"), lax.axis_index("col")
    at = jnp.stack([row, col]).astype(jnp.int32)
    limit = pltpu.CompilerParams(vmem_limit_bytes=48 * 1024 * 1024)
    call = functools.partial(pl.pallas_call, compiler_params=limit)
    turned = interaction.T
    sent_a, sent_b, ordered = call(
        first_kernel,
        out_shape=(shape(128, rows), shape(128, rows), shape(256, width)),
        in_specs=[SCALAR, WHOLE, WHOLE],
        out_specs=(WHOLE, WHOLE, WHOLE),
        cost_estimate=pl.CostEstimate(
            flops=2 * 256 * width * rows, bytes_accessed=1600000, transcendentals=0
        ),
    )(at, commands, turned)
    got_a = lax.ppermute(sent_a, "col", y_swap(1))
    got_b = lax.ppermute(sent_b, "col", y_swap(3))
    kept_a, kept_b = call(
        second_kernel,
        out_shape=(shape(128, rows), shape(128, rows)),
        in_specs=[WHOLE, WHOLE],
        out_specs=(WHOLE, WHOLE),
        cost_estimate=pl.CostEstimate(
            flops=2 * 256 * width * rows, bytes_accessed=1600000, transcendentals=0
        ),
    )(ordered, turned)
    for swap_a, swap_b in (
        (y_swap(3), y_swap(1)),
        (z_swap(1), z_swap(3)),
        (z_swap(3), z_swap(1)),
    ):
        half = kept_a.shape[0] // 2
        sent_a, sent_b = add(kept_a[half:], got_a[half:]), add(kept_b[half:], got_b[half:])
        next_a = lax.ppermute(sent_a, "col", swap_a)
        next_b = lax.ppermute(sent_b, "col", swap_b)
        kept_a, kept_b = add(kept_a[:half], got_a[:half]), add(kept_b[:half], got_b[:half])
        got_a, got_b = next_a, next_b
    summed = jnp.concatenate([kept_a, kept_b]).astype(F32) + jnp.concatenate(
        [got_a, got_b]
    ).astype(F32)
    row_mask = jnp.broadcast_to(slope_valid[:, None], (rows // SBLK, SBLK)).reshape(-1)
    slopes = (
        (residual.T.astype(F32) + summed)
        * row_mask[None, :].astype(F32)
        * frame_valid[:, None].astype(F32)
    ).astype(BF16)

    def halves(one, two, flops):
        half = one.shape[0] // 2
        return call(
            halves_kernel,
            out_shape=(shape(half, rows),) * 2,
            in_specs=[WHOLE] * 2,
            out_specs=(WHOLE,) * 2,
            cost_estimate=pl.CostEstimate(flops=flops, bytes_accessed=983040, transcendentals=0),
        )(one, two)

    left = lax.ppermute(slopes, "col", z_turn(1))
    right = lax.ppermute(slopes, "col", z_turn(-1))
    flipped = lax.ppermute(slopes, ("row", "col"), flip_pairs(0))
    pair = lax.ppermute(slopes, ("row", "col"), flip_pairs(1))
    low, high = halves(left, right, 8000000000)
    far_a = lax.ppermute(low, "col", z_turn(1))
    far_b = lax.ppermute(high, "col", z_turn(-1))
    mine, near = call(
        join_kernel,
        out_shape=(shape(128, rows), shape(64, rows)),
        in_specs=[SCALAR] + [WHOLE] * 7,
        out_specs=(WHOLE,) * 2,
    )(at, slopes, left, right, far_a, far_b, flipped, pair)
    left = lax.ppermute(mine, "col", y_turn(1))
    right = lax.ppermute(mine, "col", y_turn(-1))
    x_left = lax.ppermute(near, "row", x_turn(1))
    x_right = lax.ppermute(near, "row", x_turn(-1))
    low, high = halves(left, right, 8000000000)
    far_a = lax.ppermute(low, "col", y_turn(1))
    far_b = lax.ppermute(high, "col", y_turn(-1))
    far = call(
        stack_kernel,
        out_shape=shape(128, rows),
        in_specs=[WHOLE] * 2,
        out_specs=WHOLE,
        cost_estimate=pl.CostEstimate(flops=8000000000, bytes_accessed=983040, transcendentals=0),
    )(far_a, far_b)
    x_low, x_high = halves(x_left, x_right, 0)
    x_far_a = lax.ppermute(x_low, "row", x_turn(1))
    x_far_b = lax.ppermute(x_high, "row", x_turn(-1))
    near = call(
        gather_kernel, out_shape=shape(256, rows), in_specs=[WHOLE] * 6, out_specs=WHOLE
    )(near, x_left, x_right, x_far_a, x_far_b, low)
    other = lax.ppermute(near, "row", [(r, r ^ 1) for r in range(16)])
    return call(
        last_kernel,
        out_shape=shape(rows, rows),
        in_specs=[SCALAR] + [WHOLE] * 6,
        out_specs=pl.BlockSpec(memory_space=pl.ANY),
        scratch_shapes=[
            pltpu.VMEM((FRAMES, rows), BF16),
            pltpu.VMEM((FRAMES, rows), BF16),
            pltpu.VMEM((rows, rows), BF16),
            pltpu.SemaphoreType.DMA((len(BLOCKS),)),
        ],
        cost_estimate=pl.CostEstimate(
            flops=2 * FRAMES * rows * rows, bytes_accessed=2 * rows * rows, transcendentals=0
        ),
    )(at, mine, left, right, far, near, other)


def solution(mesh):
    placed = (P("row", "col"), P("row", "col"), P("col", None), P("row"), P("col"))
    return jax.shard_map(
        per_device, mesh=mesh, in_specs=placed, out_specs=P("row", "col"), check_vma=False
    )
```

```python
import functools

import jax
import jax.numpy as jnp
from jax import lax
from jax.experimental import pallas as pl
from jax.experimental.pallas import tpu as pltpu
from jax.sharding import PartitionSpec as P

SBLK = 128
FRAMES = 512
BF16 = jnp.bfloat16
F32 = jnp.float32
WHOLE = pl.BlockSpec(memory_space=pltpu.VMEM)
SCALAR = pl.BlockSpec(memory_space=pltpu.SMEM)


def y_swap(mask):
    return [(c, c ^ mask) for c in range(16)]


def z_swap(mask):
    return [(c, c ^ (4 * mask)) for c in range(16)]


def y_turn(by):
    return [(c, (c & 12) | ((c + by) & 3)) for c in range(16)]


def z_turn(by):
    return [(c, (c + 4 * by) & 15) for c in range(16)]


def x_turn(by):
    return [(r, (r & 9) | ((r + 2 * by) & 6)) for r in range(16)]


def flip_pairs(which):
    pairs = []
    for r in range(16):
        for c in range(16):
            z_hi, y = c >> 2, c & 3
            x = (((r >> 1) & 3) + y) & 3
            z_lo = (z_hi >> 1) ^ which
            if r >= 8 or z_lo == 0:
                pairs.append((r * 16 + c, (z_lo * 8 + x * 2 + (z_hi & 1)) * 16 + r))
    return pairs


def add(one, other):
    return (one.astype(F32) + other.astype(F32)).astype(BF16)


def shape(rows, cols):
    return jax.ShapeDtypeStruct((rows, cols), BF16)


def first_kernel(at_ref, commands_ref, interaction_ref, sent_a, sent_b, ordered_ref):
    col = at_ref[1]
    out = lax.broadcasted_iota(jnp.int32, (FRAMES, FRAMES), 0)
    src = lax.broadcasted_iota(jnp.int32, (FRAMES, FRAMES), 1)
    half = out >> 8
    low = out & 15

    def mask_of(at):
        one, two = at & 1, at >> 1
        return jnp.where(half == 0, (one << 1) | (one ^ two), at ^ two)

    piece = col ^ (mask_of((out >> 6) & 3) + 4 * mask_of((out >> 4) & 3))
    pick = (src == piece * 32 + half * 16 + low).astype(F32).astype(BF16)
    ordered = lax.dot_general(
        pick, commands_ref[...], (((1,), (1,)), ((), ())), preferred_element_type=F32
    ).astype(BF16)
    sent_a[...] = jnp.dot(
        ordered[128:256], interaction_ref[...], preferred_element_type=F32
    ).astype(BF16)
    sent_b[...] = jnp.dot(
        ordered[384:512], interaction_ref[...], preferred_element_type=F32
    ).astype(BF16)
    ordered_ref[:128] = ordered[:128]
    ordered_ref[128:] = ordered[256:384]


def second_kernel(ordered_ref, interaction_ref, kept_a, kept_b):
    kept_a[...] = jnp.dot(
        ordered_ref[:128], interaction_ref[...], preferred_element_type=F32
    ).astype(BF16)
    kept_b[...] = jnp.dot(
        ordered_ref[128:], interaction_ref[...], preferred_element_type=F32
    ).astype(BF16)


def halves_kernel(left, right, low, high):
    half = low.shape[0]
    low[...] = left[:half]
    high[...] = right[half:]


def join_kernel(at_ref, own, pair, flipped, right, left, far, mine, near):
    z = at_ref[1] >> 2
    for by, ref in ((0, own), (3, left), (1, right), (2, far)):
        mine[pl.ds(pl.multiple_of(((z + by) & 3) * 32, 32), 32)] = ref[...]
    z_lo = at_ref[0] >> 3
    near[pl.ds(pl.multiple_of(z_lo * 32, 32), 32)] = flipped[...]
    near[pl.ds(pl.multiple_of((1 - z_lo) * 32, 32), 32)] = pair[...]


def gather_kernel(near, x_left, x_right, x_far_a, x_far_b, after, out):
    first = 0
    for ref in (near, x_left, x_right, x_far_a, x_far_b):
        out[first : first + ref.shape[0]] = ref[...]
        first += ref.shape[0]


def stack_kernel(one, two, out):
    half = one.shape[0]
    out[:half] = one[...]
    out[half:] = two[...]


BLOCKS = ((0, 480), (480, 960), (960, 1440), (1440, 1760), (1760, 1920))


def last_kernel(
    at_ref,
    own,
    left,
    right,
    far,
    near,
    other,
    out,
    lhs,
    rhs,
    held,
    done,
):
    row, col = at_ref[0], at_ref[1]
    columns = held.shape[1]
    dims = (((0,), (0,)), ((), ()))

    def sent(at, source=None):
        first, end = BLOCKS[at]
        source = held.at[first:end] if source is None else source
        return pltpu.make_async_copy(source, out.at[first:end], done.at[at])

    @pl.when(row <= col)
    def _():
        y = col & 3

        for by, ref in ((0, own), (3, left), (1, right), (2, far)):
            lhs[pl.ds(pl.multiple_of(((y + by) & 3) * 128, 128), 128)] = ref[...]
        x, core = (row >> 1) & 3, row & 1
        for swap, ref in ((0, near), (1, other)):
            for at, by in enumerate((0, 3, 1, 2)):
                y_from = (x + by - (col >> 1)) & 3
                for z_lo in range(2):
                    z_from = z_lo * 2 + (core ^ swap)
                    first = pl.multiple_of(y_from * 128 + z_from * 32, 32)
                    rhs[pl.ds(first, 32)] = ref[at * 64 + z_lo * 32 : at * 64 + z_lo * 32 + 32]

    @pl.when(row < col)
    def _():
        for at, (first, end) in enumerate(BLOCKS):
            tile = lax.dot_general(lhs[:, first:end], rhs[...], dims, preferred_element_type=F32)
            held[first:end] = (tile * (1.0 / FRAMES)).astype(BF16)
            sent(at).start()

    @pl.when(row == col)
    def _():
        for at, (first, end) in enumerate(BLOCKS):
            low = first // 128 * 128
            if low:
                held[first:end, :low] = jnp.zeros((end - first, low), BF16)
            tile = lax.dot_general(
                lhs[:, first:end], rhs[:, low:], dims, preferred_element_type=F32
            ) * (1.0 / FRAMES)
            down = lax.broadcasted_iota(jnp.int32, tile.shape, 0) + first
            across = lax.broadcasted_iota(jnp.int32, tile.shape, 1) + low
            held[first:end, low:] = jnp.where(down <= across, tile, 0.0).astype(BF16)
            sent(at).start()

    @pl.when(row > col)
    def _():
        held[:480] = jnp.zeros((480, columns), BF16)
        for at, (first, end) in enumerate(BLOCKS):
            sent(at, held.at[: end - first]).start()

    for at in range(len(BLOCKS)):
        sent(at).wait()


def per_device(residual, interaction, commands, slope_valid, frame_valid):
    rows, width = interaction.shape
    row, col = lax.axis_index("row"), lax.axis_index("col")
    at = jnp.stack([row, col]).astype(jnp.int32)
    limit = pltpu.CompilerParams(vmem_limit_bytes=48 * 1024 * 1024)
    call = functools.partial(pl.pallas_call, compiler_params=limit)
    turned = interaction.T
    sent_a, sent_b, ordered = call(
        first_kernel,
        out_shape=(shape(128, rows), shape(128, rows), shape(256, width)),
        in_specs=[SCALAR, WHOLE, WHOLE],
        out_specs=(WHOLE, WHOLE, WHOLE),
        cost_estimate=pl.CostEstimate(
            flops=2 * 256 * width * rows, bytes_accessed=1600000, transcendentals=0
        ),
    )(at, commands, turned)
    got_a = lax.ppermute(sent_a, "col", y_swap(1))
    got_b = lax.ppermute(sent_b, "col", y_swap(3))
    kept_a, kept_b = call(
        second_kernel,
        out_shape=(shape(128, rows), shape(128, rows)),
        in_specs=[WHOLE, WHOLE],
        out_specs=(WHOLE, WHOLE),
        cost_estimate=pl.CostEstimate(
            flops=2 * 256 * width * rows, bytes_accessed=1600000, transcendentals=0
        ),
    )(ordered, turned)
    for swap_a, swap_b in (
        (y_swap(3), y_swap(1)),
        (z_swap(1), z_swap(3)),
        (z_swap(3), z_swap(1)),
    ):
        half = kept_a.shape[0] // 2
        sent_a, sent_b = add(kept_a[half:], got_a[half:]), add(kept_b[half:], got_b[half:])
        next_a = lax.ppermute(sent_a, "col", swap_a)
        next_b = lax.ppermute(sent_b, "col", swap_b)
        kept_a, kept_b = add(kept_a[:half], got_a[:half]), add(kept_b[:half], got_b[:half])
        got_a, got_b = next_a, next_b
    summed = jnp.concatenate([kept_a, kept_b]).astype(F32) + jnp.concatenate(
        [got_a, got_b]
    ).astype(F32)
    row_mask = jnp.broadcast_to(slope_valid[:, None], (rows // SBLK, SBLK)).reshape(-1)
    slopes = (
        (residual.T.astype(F32) + summed)
        * row_mask[None, :].astype(F32)
        * frame_valid[:, None].astype(F32)
    ).astype(BF16)

    def halves(one, two, flops):
        half = one.shape[0] // 2
        return call(
            halves_kernel,
            out_shape=(shape(half, rows),) * 2,
            in_specs=[WHOLE] * 2,
            out_specs=(WHOLE,) * 2,
            cost_estimate=pl.CostEstimate(flops=flops, bytes_accessed=983040, transcendentals=0),
        )(one, two)

    pair = lax.ppermute(slopes, ("row", "col"), flip_pairs(1))
    flipped = lax.ppermute(slopes, ("row", "col"), flip_pairs(0))
    left = lax.ppermute(slopes, "col", z_turn(1))
    right = lax.ppermute(slopes, "col", z_turn(-1))
    far = lax.ppermute(slopes, "col", z_turn(2))
    mine, near = call(
        join_kernel,
        out_shape=(shape(128, rows), shape(64, rows)),
        in_specs=[SCALAR] + [WHOLE] * 6,
        out_specs=(WHOLE,) * 2,
    )(at, slopes, pair, flipped, right, left, far)
    left = lax.ppermute(mine, "col", y_turn(1))
    right = lax.ppermute(mine, "col", y_turn(-1))
    x_left = lax.ppermute(near, "row", x_turn(1))
    x_right = lax.ppermute(near, "row", x_turn(-1))
    low, high = halves(left, right, 8000000000)
    far_a = lax.ppermute(low, "col", y_turn(1))
    far_b = lax.ppermute(high, "col", y_turn(-1))
    far = call(
        stack_kernel,
        out_shape=shape(128, rows),
        in_specs=[WHOLE] * 2,
        out_specs=WHOLE,
        cost_estimate=pl.CostEstimate(flops=8000000000, bytes_accessed=983040, transcendentals=0),
    )(far_a, far_b)
    x_low, x_high = halves(x_left, x_right, 0)
    x_far_a = lax.ppermute(x_low, "row", x_turn(1))
    x_far_b = lax.ppermute(x_high, "row", x_turn(-1))
    near = call(
        gather_kernel, out_shape=shape(256, rows), in_specs=[WHOLE] * 6, out_specs=WHOLE
    )(near, x_left, x_right, x_far_a, x_far_b, low)
    other = lax.ppermute(near, "row", [(r, r ^ 1) for r in range(16)])
    return call(
        last_kernel,
        out_shape=shape(rows, rows),
        in_specs=[SCALAR] + [WHOLE] * 6,
        out_specs=pl.BlockSpec(memory_space=pl.ANY),
        scratch_shapes=[
            pltpu.VMEM((FRAMES, rows), BF16),
            pltpu.VMEM((FRAMES, rows), BF16),
            pltpu.VMEM((rows, rows), BF16),
            pltpu.SemaphoreType.DMA((len(BLOCKS),)),
        ],
        cost_estimate=pl.CostEstimate(
            flops=2 * FRAMES * rows * rows, bytes_accessed=2 * rows * rows, transcendentals=0
        ),
    )(at, mine, left, right, far, near, other)


def solution(mesh):
    placed = (P("row", "col"), P("row", "col"), P("col", None), P("row"), P("col"))
    return jax.shard_map(
        per_device, mesh=mesh, in_specs=placed, out_specs=P("row", "col"), check_vma=False
    )
```

```python
import functools

import jax
import jax.numpy as jnp
from jax import lax
from jax.experimental import pallas as pl
from jax.experimental.pallas import tpu as pltpu
from jax.sharding import PartitionSpec as P

SBLK = 128
FRAMES = 512
BF16 = jnp.bfloat16
F32 = jnp.float32
WHOLE = pl.BlockSpec(memory_space=pltpu.VMEM)
SCALAR = pl.BlockSpec(memory_space=pltpu.SMEM)


def y_swap(mask):
    return [(c, c ^ mask) for c in range(16)]


def z_swap(mask):
    return [(c, c ^ (4 * mask)) for c in range(16)]


def y_turn(by):
    return [(c, (c & 12) | ((c + by) & 3)) for c in range(16)]


def z_turn(by):
    return [(c, (c + 4 * by) & 15) for c in range(16)]


def x_turn(by):
    return [(r, (r & 9) | ((r + 2 * by) & 6)) for r in range(16)]


def flip_pairs():
    pairs = []
    for r in range(16):
        for c in range(16):
            z_hi, y = c >> 2, c & 3
            x = (((r >> 1) & 3) + y) & 3
            to = (z_hi >> 1) * 8 + x * 2 + (z_hi & 1)
            pairs.append((r * 16 + c, to * 16 + r))
    return pairs


def add(one, other):
    return (one.astype(F32) + other.astype(F32)).astype(BF16)


def shape(rows, cols):
    return jax.ShapeDtypeStruct((rows, cols), BF16)


def first_kernel(at_ref, commands_ref, interaction_ref, sent_a, sent_b, ordered_ref):
    col = at_ref[1]
    out = lax.broadcasted_iota(jnp.int32, (FRAMES, FRAMES), 0)
    src = lax.broadcasted_iota(jnp.int32, (FRAMES, FRAMES), 1)
    half = out >> 8
    low = out & 15

    def mask_of(at):
        one, two = at & 1, at >> 1
        return jnp.where(half == 0, (one << 1) | (one ^ two), at ^ two)

    piece = col ^ (mask_of((out >> 6) & 3) + 4 * mask_of((out >> 4) & 3))
    pick = (src == piece * 32 + half * 16 + low).astype(F32).astype(BF16)
    ordered = lax.dot_general(
        pick, commands_ref[...], (((1,), (1,)), ((), ())), preferred_element_type=F32
    ).astype(BF16)
    sent_a[...] = jnp.dot(
        ordered[128:256], interaction_ref[...], preferred_element_type=F32
    ).astype(BF16)
    sent_b[...] = jnp.dot(
        ordered[384:512], interaction_ref[...], preferred_element_type=F32
    ).astype(BF16)
    ordered_ref[:128] = ordered[:128]
    ordered_ref[128:] = ordered[256:384]


def second_kernel(ordered_ref, interaction_ref, kept_a, kept_b):
    kept_a[...] = jnp.dot(
        ordered_ref[:128], interaction_ref[...], preferred_element_type=F32
    ).astype(BF16)
    kept_b[...] = jnp.dot(
        ordered_ref[128:], interaction_ref[...], preferred_element_type=F32
    ).astype(BF16)


def halves_kernel(left, right, low, high):
    half = low.shape[0]
    low[...] = left[:half]
    high[...] = right[half:]


def z_join_kernel(at_ref, own, left, right, far_a, far_b, mine):
    z = at_ref[1] >> 2

    def put(by, start, ref):
        first = pl.multiple_of(((z + by) & 3) * 32 + start, 16)
        mine[pl.ds(first, ref.shape[0])] = ref[...]

    put(0, 0, own)
    put(3, 0, left)
    put(1, 0, right)
    put(2, 0, far_a)
    put(2, 16, far_b)


def pair_join_kernel(at_ref, flipped, pair, near):
    z_lo = at_ref[0] >> 3
    near[pl.ds(pl.multiple_of(z_lo * 32, 32), 32)] = flipped[...]
    near[pl.ds(pl.multiple_of((1 - z_lo) * 32, 32), 32)] = pair[...]


def gather_kernel(near, x_left, x_right, x_far_a, x_far_b, after, out):
    first = 0
    for ref in (near, x_left, x_right, x_far_a, x_far_b):
        out[first : first + ref.shape[0]] = ref[...]
        first += ref.shape[0]


def stack_kernel(one, two, out):
    half = one.shape[0]
    out[:half] = one[...]
    out[half:] = two[...]


BLOCKS = ((0, 480), (480, 960), (960, 1440), (1440, 1760), (1760, 1920))


def last_kernel(
    at_ref,
    own,
    left,
    right,
    far,
    near,
    other,
    out,
    lhs,
    rhs,
    held,
    done,
):
    row, col = at_ref[0], at_ref[1]
    columns = held.shape[1]
    dims = (((0,), (0,)), ((), ()))

    def sent(at, source=None):
        first, end = BLOCKS[at]
        source = held.at[first:end] if source is None else source
        return pltpu.make_async_copy(source, out.at[first:end], done.at[at])

    @pl.when(row <= col)
    def _():
        y = col & 3

        for by, ref in ((0, own), (3, left), (1, right), (2, far)):
            lhs[pl.ds(pl.multiple_of(((y + by) & 3) * 128, 128), 128)] = ref[...]
        x, core = (row >> 1) & 3, row & 1
        for swap, ref in ((0, near), (1, other)):
            for at, by in enumerate((0, 3, 1, 2)):
                y_from = (x + by - (col >> 1)) & 3
                for z_lo in range(2):
                    z_from = z_lo * 2 + (core ^ swap)
                    first = pl.multiple_of(y_from * 128 + z_from * 32, 32)
                    rhs[pl.ds(first, 32)] = ref[at * 64 + z_lo * 32 : at * 64 + z_lo * 32 + 32]

    @pl.when(row < col)
    def _():
        for at, (first, end) in enumerate(BLOCKS):
            tile = lax.dot_general(lhs[:, first:end], rhs[...], dims, preferred_element_type=F32)
            held[first:end] = (tile * (1.0 / FRAMES)).astype(BF16)
            sent(at).start()

    @pl.when(row == col)
    def _():
        for at, (first, end) in enumerate(BLOCKS):
            low = first // 128 * 128
            if low:
                held[first:end, :low] = jnp.zeros((end - first, low), BF16)
            tile = lax.dot_general(
                lhs[:, first:end], rhs[:, low:], dims, preferred_element_type=F32
            ) * (1.0 / FRAMES)
            down = lax.broadcasted_iota(jnp.int32, tile.shape, 0) + first
            across = lax.broadcasted_iota(jnp.int32, tile.shape, 1) + low
            held[first:end, low:] = jnp.where(down <= across, tile, 0.0).astype(BF16)
            sent(at).start()

    @pl.when(row > col)
    def _():
        held[:480] = jnp.zeros((480, columns), BF16)
        for at, (first, end) in enumerate(BLOCKS):
            sent(at, held.at[: end - first]).start()

    for at in range(len(BLOCKS)):
        sent(at).wait()


def per_device(residual, interaction, commands, slope_valid, frame_valid):
    rows, width = interaction.shape
    row, col = lax.axis_index("row"), lax.axis_index("col")
    at = jnp.stack([row, col]).astype(jnp.int32)
    limit = pltpu.CompilerParams(vmem_limit_bytes=48 * 1024 * 1024)
    call = functools.partial(pl.pallas_call, compiler_params=limit)
    turned = interaction.T
    sent_a, sent_b, ordered = call(
        first_kernel,
        out_shape=(shape(128, rows), shape(128, rows), shape(256, width)),
        in_specs=[SCALAR, WHOLE, WHOLE],
        out_specs=(WHOLE, WHOLE, WHOLE),
        cost_estimate=pl.CostEstimate(
            flops=2 * 256 * width * rows, bytes_accessed=1600000, transcendentals=0
        ),
    )(at, commands, turned)
    got_a = lax.ppermute(sent_a, "col", y_swap(1))
    got_b = lax.ppermute(sent_b, "col", y_swap(3))
    kept_a, kept_b = call(
        second_kernel,
        out_shape=(shape(128, rows), shape(128, rows)),
        in_specs=[WHOLE, WHOLE],
        out_specs=(WHOLE, WHOLE),
        cost_estimate=pl.CostEstimate(
            flops=2 * 256 * width * rows, bytes_accessed=1600000, transcendentals=0
        ),
    )(ordered, turned)
    for swap_a, swap_b in (
        (y_swap(3), y_swap(1)),
        (z_swap(1), z_swap(3)),
        (z_swap(3), z_swap(1)),
    ):
        half = kept_a.shape[0] // 2
        sent_a, sent_b = add(kept_a[half:], got_a[half:]), add(kept_b[half:], got_b[half:])
        next_a = lax.ppermute(sent_a, "col", swap_a)
        next_b = lax.ppermute(sent_b, "col", swap_b)
        kept_a, kept_b = add(kept_a[:half], got_a[:half]), add(kept_b[:half], got_b[:half])
        got_a, got_b = next_a, next_b
    summed = jnp.concatenate([kept_a, kept_b]).astype(F32) + jnp.concatenate(
        [got_a, got_b]
    ).astype(F32)
    row_mask = jnp.broadcast_to(slope_valid[:, None], (rows // SBLK, SBLK)).reshape(-1)
    slopes = (
        (residual.T.astype(F32) + summed)
        * row_mask[None, :].astype(F32)
        * frame_valid[:, None].astype(F32)
    ).astype(BF16)

    def halves(one, two, flops):
        half = one.shape[0] // 2
        return call(
            halves_kernel,
            out_shape=(shape(half, rows),) * 2,
            in_specs=[WHOLE] * 2,
            out_specs=(WHOLE,) * 2,
            cost_estimate=pl.CostEstimate(flops=flops, bytes_accessed=983040, transcendentals=0),
        )(one, two)

    left = lax.ppermute(slopes, "col", z_turn(1))
    right = lax.ppermute(slopes, "col", z_turn(-1))
    flipped = lax.ppermute(slopes, ("row", "col"), flip_pairs())
    low, high = halves(left, right, 8000000000)
    far_a = lax.ppermute(low, "col", z_turn(1))
    far_b = lax.ppermute(high, "col", z_turn(-1))
    mine = call(
        z_join_kernel,
        out_shape=shape(128, rows),
        in_specs=[SCALAR] + [WHOLE] * 5,
        out_specs=WHOLE,
    )(at, slopes, left, right, far_a, far_b)
    left = lax.ppermute(mine, "col", y_turn(1))
    right = lax.ppermute(mine, "col", y_turn(-1))
    pair = lax.ppermute(flipped, "row", [(r, r ^ 8) for r in range(16)])
    near = call(
        pair_join_kernel,
        out_shape=shape(64, rows),
        in_specs=[SCALAR] + [WHOLE] * 2,
        out_specs=WHOLE,
        cost_estimate=pl.CostEstimate(flops=4000000000, bytes_accessed=491520, transcendentals=0),
    )(at, flipped, pair)
    x_left = lax.ppermute(near, "row", x_turn(1))
    x_right = lax.ppermute(near, "row", x_turn(-1))
    low, high = halves(left, right, 16000000000)
    far_a = lax.ppermute(low, "col", y_turn(1))
    far_b = lax.ppermute(high, "col", y_turn(-1))
    far = call(
        stack_kernel,
        out_shape=shape(128, rows),
        in_specs=[WHOLE] * 2,
        out_specs=WHOLE,
        cost_estimate=pl.CostEstimate(flops=16000000000, bytes_accessed=983040, transcendentals=0),
    )(far_a, far_b)
    x_low, x_high = halves(x_left, x_right, 0)
    x_far_a = lax.ppermute(x_low, "row", x_turn(1))
    x_far_b = lax.ppermute(x_high, "row", x_turn(-1))
    near = call(
        gather_kernel, out_shape=shape(256, rows), in_specs=[WHOLE] * 6, out_specs=WHOLE
    )(near, x_left, x_right, x_far_a, x_far_b, low)
    other = lax.ppermute(near, "row", [(r, r ^ 1) for r in range(16)])
    return call(
        last_kernel,
        out_shape=shape(rows, rows),
        in_specs=[SCALAR] + [WHOLE] * 6,
        out_specs=pl.BlockSpec(memory_space=pl.ANY),
        scratch_shapes=[
            pltpu.VMEM((FRAMES, rows), BF16),
            pltpu.VMEM((FRAMES, rows), BF16),
            pltpu.VMEM((rows, rows), BF16),
            pltpu.SemaphoreType.DMA((len(BLOCKS),)),
        ],
        cost_estimate=pl.CostEstimate(
            flops=2 * FRAMES * rows * rows, bytes_accessed=2 * rows * rows, transcendentals=0
        ),
    )(at, mine, left, right, far, near, other)


def solution(mesh):
    placed = (P("row", "col"), P("row", "col"), P("col", None), P("row"), P("col"))
    return jax.shard_map(
        per_device, mesh=mesh, in_specs=placed, out_specs=P("row", "col"), check_vma=False
    )
```

```python
import functools

import jax
import jax.numpy as jnp
from jax import lax
from jax.experimental import pallas as pl
from jax.experimental.pallas import tpu as pltpu
from jax.sharding import PartitionSpec as P

SBLK = 128
FRAMES = 512
BF16 = jnp.bfloat16
F32 = jnp.float32
WHOLE = pl.BlockSpec(memory_space=pltpu.VMEM)
SCALAR = pl.BlockSpec(memory_space=pltpu.SMEM)


def y_swap(mask):
    return [(c, c ^ mask) for c in range(16)]


def z_swap(mask):
    return [(c, c ^ (4 * mask)) for c in range(16)]


def y_turn(by):
    return [(c, (c & 12) | ((c + by) & 3)) for c in range(16)]


def z_turn(by):
    return [(c, (c + 4 * by) & 15) for c in range(16)]


def x_turn(by):
    return [(r, (r & 9) | ((r + 2 * by) & 6)) for r in range(16)]


def flip_pairs():
    pairs = []
    for r in range(16):
        for c in range(16):
            z_hi, y = c >> 2, c & 3
            x = (((r >> 1) & 3) + y) & 3
            to = (z_hi >> 1) * 8 + x * 2 + (z_hi & 1)
            pairs.append((r * 16 + c, to * 16 + r))
    return pairs


def add(one, other):
    return (one.astype(F32) + other.astype(F32)).astype(BF16)


def shape(rows, cols):
    return jax.ShapeDtypeStruct((rows, cols), BF16)


def first_kernel(at_ref, commands_ref, interaction_ref, sent_a, sent_b, ordered_ref):
    col = at_ref[1]
    out = lax.broadcasted_iota(jnp.int32, (FRAMES, FRAMES), 0)
    src = lax.broadcasted_iota(jnp.int32, (FRAMES, FRAMES), 1)
    half = out >> 8
    low = out & 15

    def mask_of(at):
        one, two = at & 1, at >> 1
        return jnp.where(half == 0, (one << 1) | (one ^ two), at ^ two)

    piece = col ^ (mask_of((out >> 6) & 3) + 4 * mask_of((out >> 4) & 3))
    pick = (src == piece * 32 + half * 16 + low).astype(F32).astype(BF16)
    ordered = lax.dot_general(
        pick, commands_ref[...], (((1,), (1,)), ((), ())), preferred_element_type=F32
    ).astype(BF16)
    sent_a[...] = jnp.dot(
        ordered[128:256], interaction_ref[...], preferred_element_type=F32
    ).astype(BF16)
    sent_b[...] = jnp.dot(
        ordered[384:512], interaction_ref[...], preferred_element_type=F32
    ).astype(BF16)
    ordered_ref[:128] = ordered[:128]
    ordered_ref[128:] = ordered[256:384]


def second_kernel(ordered_ref, interaction_ref, kept_a, kept_b):
    kept_a[...] = jnp.dot(
        ordered_ref[:128], interaction_ref[...], preferred_element_type=F32
    ).astype(BF16)
    kept_b[...] = jnp.dot(
        ordered_ref[128:], interaction_ref[...], preferred_element_type=F32
    ).astype(BF16)


def halves_kernel(left, right, low, high):
    half = low.shape[0]
    low[...] = left[:half]
    high[...] = right[half:]


def z_join_kernel(at_ref, own, left, right, far_a, far_b, mine):
    z = at_ref[1] >> 2

    def put(by, start, ref):
        first = pl.multiple_of(((z + by) & 3) * 32 + start, 16)
        mine[pl.ds(first, ref.shape[0])] = ref[...]

    put(0, 0, own)
    put(3, 0, left)
    put(1, 0, right)
    put(2, 0, far_a)
    put(2, 16, far_b)


def pair_join_kernel(at_ref, flipped, pair, near):
    z_lo = at_ref[0] >> 3
    near[pl.ds(pl.multiple_of(z_lo * 32, 32), 32)] = flipped[...]
    near[pl.ds(pl.multiple_of((1 - z_lo) * 32, 32), 32)] = pair[...]


def gather_kernel(near, x_left, x_right, x_far_a, x_far_b, after, out):
    first = 0
    for ref in (near, x_left, x_right, x_far_a, x_far_b):
        out[first : first + ref.shape[0]] = ref[...]
        first += ref.shape[0]


def stack_kernel(one, two, out):
    half = one.shape[0]
    out[:half] = one[...]
    out[half:] = two[...]


BLOCKS = ((0, 480), (480, 960), (960, 1440), (1440, 1760), (1760, 1920))


def last_kernel(
    at_ref,
    own,
    left,
    right,
    far,
    near,
    other,
    out,
    lhs,
    rhs,
    held,
    done,
):
    row, col = at_ref[0], at_ref[1]
    columns = held.shape[1]
    dims = (((0,), (0,)), ((), ()))

    def sent(at, source=None):
        first, end = BLOCKS[at]
        source = held.at[first:end] if source is None else source
        return pltpu.make_async_copy(source, out.at[first:end], done.at[at])

    @pl.when(row <= col)
    def _():
        y = col & 3

        for by, ref in ((0, own), (3, left), (1, right), (2, far)):
            lhs[pl.ds(pl.multiple_of(((y + by) & 3) * 128, 128), 128)] = ref[...]
        x, core = (row >> 1) & 3, row & 1
        for swap, ref in ((0, near), (1, other)):
            for at, by in enumerate((0, 3, 1, 2)):
                y_from = (x + by - (col >> 1)) & 3
                for z_lo in range(2):
                    z_from = z_lo * 2 + (core ^ swap)
                    first = pl.multiple_of(y_from * 128 + z_from * 32, 32)
                    rhs[pl.ds(first, 32)] = ref[at * 64 + z_lo * 32 : at * 64 + z_lo * 32 + 32]

    @pl.when(row < col)
    def _():
        for at, (first, end) in enumerate(BLOCKS):
            tile = lax.dot_general(lhs[:, first:end], rhs[...], dims, preferred_element_type=F32)
            held[first:end] = (tile * (1.0 / FRAMES)).astype(BF16)
            sent(at).start()

    @pl.when(row == col)
    def _():
        for at, (first, end) in enumerate(BLOCKS):
            low = first // 128 * 128
            if low:
                held[first:end, :low] = jnp.zeros((end - first, low), BF16)
            tile = lax.dot_general(
                lhs[:, first:end], rhs[:, low:], dims, preferred_element_type=F32
            ) * (1.0 / FRAMES)
            down = lax.broadcasted_iota(jnp.int32, tile.shape, 0) + first
            across = lax.broadcasted_iota(jnp.int32, tile.shape, 1) + low
            held[first:end, low:] = jnp.where(down <= across, tile, 0.0).astype(BF16)
            sent(at).start()

    @pl.when(row > col)
    def _():
        held[:480] = jnp.zeros((480, columns), BF16)
        for at, (first, end) in enumerate(BLOCKS):
            sent(at, held.at[: end - first]).start()

    for at in range(len(BLOCKS)):
        sent(at).wait()


def per_device(residual, interaction, commands, slope_valid, frame_valid):
    rows, width = interaction.shape
    row, col = lax.axis_index("row"), lax.axis_index("col")
    at = jnp.stack([row, col]).astype(jnp.int32)
    limit = pltpu.CompilerParams(vmem_limit_bytes=48 * 1024 * 1024)
    call = functools.partial(pl.pallas_call, compiler_params=limit)
    turned = interaction.T
    sent_a, sent_b, ordered = call(
        first_kernel,
        out_shape=(shape(128, rows), shape(128, rows), shape(256, width)),
        in_specs=[SCALAR, WHOLE, WHOLE],
        out_specs=(WHOLE, WHOLE, WHOLE),
        cost_estimate=pl.CostEstimate(
            flops=2 * 256 * width * rows, bytes_accessed=1600000, transcendentals=0
        ),
    )(at, commands, turned)
    got_a = lax.ppermute(sent_a, "col", y_swap(1))
    got_b = lax.ppermute(sent_b, "col", y_swap(3))
    kept_a, kept_b = call(
        second_kernel,
        out_shape=(shape(128, rows), shape(128, rows)),
        in_specs=[WHOLE, WHOLE],
        out_specs=(WHOLE, WHOLE),
        cost_estimate=pl.CostEstimate(
            flops=2 * 256 * width * rows, bytes_accessed=1600000, transcendentals=0
        ),
    )(ordered, turned)
    for swap_a, swap_b in (
        (y_swap(3), y_swap(1)),
        (z_swap(1), z_swap(3)),
        (z_swap(3), z_swap(1)),
    ):
        half = kept_a.shape[0] // 2
        sent_a, sent_b = add(kept_a[half:], got_a[half:]), add(kept_b[half:], got_b[half:])
        next_a = lax.ppermute(sent_a, "col", swap_a)
        next_b = lax.ppermute(sent_b, "col", swap_b)
        kept_a, kept_b = add(kept_a[:half], got_a[:half]), add(kept_b[:half], got_b[:half])
        got_a, got_b = next_a, next_b
    summed = jnp.concatenate([kept_a, kept_b]).astype(F32) + jnp.concatenate(
        [got_a, got_b]
    ).astype(F32)
    row_mask = jnp.broadcast_to(slope_valid[:, None], (rows // SBLK, SBLK)).reshape(-1)
    slopes = (
        (residual.T.astype(F32) + summed)
        * row_mask[None, :].astype(F32)
        * frame_valid[:, None].astype(F32)
    ).astype(BF16)

    def halves(one, two, flops):
        half = one.shape[0] // 2
        return call(
            halves_kernel,
            out_shape=(shape(half, rows),) * 2,
            in_specs=[WHOLE] * 2,
            out_specs=(WHOLE,) * 2,
            cost_estimate=pl.CostEstimate(flops=flops, bytes_accessed=983040, transcendentals=0),
        )(one, two)

    left = lax.ppermute(slopes, "col", z_turn(1))
    right = lax.ppermute(slopes, "col", z_turn(-1))
    flipped = lax.ppermute(slopes, ("row", "col"), flip_pairs())
    low, high = halves(left, right, 8000000000)
    far_a = lax.ppermute(low, "col", z_turn(1))
    far_b = lax.ppermute(high, "col", z_turn(-1))
    mine = call(
        z_join_kernel,
        out_shape=shape(128, rows),
        in_specs=[SCALAR] + [WHOLE] * 5,
        out_specs=WHOLE,
    )(at, slopes, left, right, far_a, far_b)
    left = lax.ppermute(mine, "col", y_turn(1))
    right = lax.ppermute(mine, "col", y_turn(-1))
    pair = lax.ppermute(flipped, "row", [(r, r ^ 8) for r in range(16)])
    near = call(
        pair_join_kernel,
        out_shape=shape(64, rows),
        in_specs=[SCALAR] + [WHOLE] * 2,
        out_specs=WHOLE,
        cost_estimate=pl.CostEstimate(flops=1600000000, bytes_accessed=491520, transcendentals=0),
    )(at, flipped, pair)
    x_left = lax.ppermute(near, "row", x_turn(1))
    x_right = lax.ppermute(near, "row", x_turn(-1))
    low, high = halves(left, right, 8000000000)
    far_a = lax.ppermute(low, "col", y_turn(1))
    far_b = lax.ppermute(high, "col", y_turn(-1))
    far = call(
        stack_kernel,
        out_shape=shape(128, rows),
        in_specs=[WHOLE] * 2,
        out_specs=WHOLE,
        cost_estimate=pl.CostEstimate(flops=8000000000, bytes_accessed=983040, transcendentals=0),
    )(far_a, far_b)
    x_low, x_high = halves(x_left, x_right, 0)
    x_far_a = lax.ppermute(x_low, "row", x_turn(1))
    x_far_b = lax.ppermute(x_high, "row", x_turn(-1))
    near = call(
        gather_kernel, out_shape=shape(256, rows), in_specs=[WHOLE] * 6, out_specs=WHOLE
    )(near, x_left, x_right, x_far_a, x_far_b, low)
    other = lax.ppermute(near, "row", [(r, r ^ 1) for r in range(16)])
    return call(
        last_kernel,
        out_shape=shape(rows, rows),
        in_specs=[SCALAR] + [WHOLE] * 6,
        out_specs=pl.BlockSpec(memory_space=pl.ANY),
        scratch_shapes=[
            pltpu.VMEM((FRAMES, rows), BF16),
            pltpu.VMEM((FRAMES, rows), BF16),
            pltpu.VMEM((rows, rows), BF16),
            pltpu.SemaphoreType.DMA((len(BLOCKS),)),
        ],
        cost_estimate=pl.CostEstimate(
            flops=2 * FRAMES * rows * rows, bytes_accessed=2 * rows * rows, transcendentals=0
        ),
    )(at, mine, left, right, far, near, other)


def solution(mesh):
    placed = (P("row", "col"), P("row", "col"), P("col", None), P("row"), P("col"))
    return jax.shard_map(
        per_device, mesh=mesh, in_specs=placed, out_specs=P("row", "col"), check_vma=False
    )
```

```python
import functools

import jax
import jax.numpy as jnp
from jax import lax
from jax.experimental import pallas as pl
from jax.experimental.pallas import tpu as pltpu
from jax.sharding import PartitionSpec as P

SBLK = 128
FRAMES = 512
BF16 = jnp.bfloat16
F32 = jnp.float32
WHOLE = pl.BlockSpec(memory_space=pltpu.VMEM)
SCALAR = pl.BlockSpec(memory_space=pltpu.SMEM)


def y_swap(mask):
    return [(c, c ^ mask) for c in range(16)]


def z_swap(mask):
    return [(c, c ^ (4 * mask)) for c in range(16)]


def y_turn(by):
    return [(c, (c & 12) | ((c + by) & 3)) for c in range(16)]


def z_turn(by):
    return [(c, (c + 4 * by) & 15) for c in range(16)]


def x_turn(by):
    return [(r, (r & 9) | ((r + 2 * by) & 6)) for r in range(16)]


def flip_pairs():
    pairs = []
    for r in range(16):
        for c in range(16):
            z_hi, y = c >> 2, c & 3
            x = (((r >> 1) & 3) + y) & 3
            to = (z_hi >> 1) * 8 + x * 2 + (z_hi & 1)
            pairs.append((r * 16 + c, to * 16 + r))
    return pairs


def add(one, other):
    return (one.astype(F32) + other.astype(F32)).astype(BF16)


def shape(rows, cols):
    return jax.ShapeDtypeStruct((rows, cols), BF16)


def first_kernel(at_ref, commands_ref, interaction_ref, sent_a, sent_b, ordered_ref):
    col = at_ref[1]
    out = lax.broadcasted_iota(jnp.int32, (FRAMES, FRAMES), 0)
    src = lax.broadcasted_iota(jnp.int32, (FRAMES, FRAMES), 1)
    half = out >> 8
    low = out & 15

    def mask_of(at):
        one, two = at & 1, at >> 1
        return jnp.where(half == 0, (one << 1) | (one ^ two), at ^ two)

    piece = col ^ (mask_of((out >> 6) & 3) + 4 * mask_of((out >> 4) & 3))
    pick = (src == piece * 32 + half * 16 + low).astype(F32).astype(BF16)
    ordered = lax.dot_general(
        pick, commands_ref[...], (((1,), (1,)), ((), ())), preferred_element_type=F32
    ).astype(BF16)
    sent_a[...] = jnp.dot(
        ordered[128:256], interaction_ref[...], preferred_element_type=F32
    ).astype(BF16)
    sent_b[...] = jnp.dot(
        ordered[384:512], interaction_ref[...], preferred_element_type=F32
    ).astype(BF16)
    ordered_ref[:128] = ordered[:128]
    ordered_ref[128:] = ordered[256:384]


def second_kernel(ordered_ref, interaction_ref, kept_a, kept_b):
    kept_a[...] = jnp.dot(
        ordered_ref[:128], interaction_ref[...], preferred_element_type=F32
    ).astype(BF16)
    kept_b[...] = jnp.dot(
        ordered_ref[128:], interaction_ref[...], preferred_element_type=F32
    ).astype(BF16)


def halves_kernel(left, right, low, high):
    half = low.shape[0]
    low[...] = left[:half]
    high[...] = right[half:]


def z_join_kernel(at_ref, own, right, left, far, mine):
    z = at_ref[1] >> 2
    for by, ref in ((0, own), (3, left), (1, right), (2, far)):
        mine[pl.ds(pl.multiple_of(((z + by) & 3) * 32, 32), 32)] = ref[...]


def pair_join_kernel(at_ref, flipped, pair, near):
    z_lo = at_ref[0] >> 3
    near[pl.ds(pl.multiple_of(z_lo * 32, 32), 32)] = flipped[...]
    near[pl.ds(pl.multiple_of((1 - z_lo) * 32, 32), 32)] = pair[...]


def gather_kernel(near, x_left, x_right, x_far_a, x_far_b, after, out):
    first = 0
    for ref in (near, x_left, x_right, x_far_a, x_far_b):
        out[first : first + ref.shape[0]] = ref[...]
        first += ref.shape[0]


def stack_kernel(one, two, out):
    half = one.shape[0]
    out[:half] = one[...]
    out[half:] = two[...]


BLOCKS = ((0, 480), (480, 960), (960, 1440), (1440, 1760), (1760, 1920))


def last_kernel(
    at_ref,
    own,
    left,
    right,
    far,
    near,
    other,
    out,
    lhs,
    rhs,
    held,
    done,
):
    row, col = at_ref[0], at_ref[1]
    columns = held.shape[1]
    dims = (((0,), (0,)), ((), ()))

    def sent(at, source=None):
        first, end = BLOCKS[at]
        source = held.at[first:end] if source is None else source
        return pltpu.make_async_copy(source, out.at[first:end], done.at[at])

    @pl.when(row <= col)
    def _():
        y = col & 3

        for by, ref in ((0, own), (3, left), (1, right), (2, far)):
            lhs[pl.ds(pl.multiple_of(((y + by) & 3) * 128, 128), 128)] = ref[...]
        x, core = (row >> 1) & 3, row & 1
        for swap, ref in ((0, near), (1, other)):
            for at, by in enumerate((0, 3, 1, 2)):
                y_from = (x + by - (col >> 1)) & 3
                for z_lo in range(2):
                    z_from = z_lo * 2 + (core ^ swap)
                    first = pl.multiple_of(y_from * 128 + z_from * 32, 32)
                    rhs[pl.ds(first, 32)] = ref[at * 64 + z_lo * 32 : at * 64 + z_lo * 32 + 32]

    @pl.when(row < col)
    def _():
        for at, (first, end) in enumerate(BLOCKS):
            tile = lax.dot_general(lhs[:, first:end], rhs[...], dims, preferred_element_type=F32)
            held[first:end] = (tile * (1.0 / FRAMES)).astype(BF16)
            sent(at).start()

    @pl.when(row == col)
    def _():
        for at, (first, end) in enumerate(BLOCKS):
            low = first // 128 * 128
            if low:
                held[first:end, :low] = jnp.zeros((end - first, low), BF16)
            tile = lax.dot_general(
                lhs[:, first:end], rhs[:, low:], dims, preferred_element_type=F32
            ) * (1.0 / FRAMES)
            down = lax.broadcasted_iota(jnp.int32, tile.shape, 0) + first
            across = lax.broadcasted_iota(jnp.int32, tile.shape, 1) + low
            held[first:end, low:] = jnp.where(down <= across, tile, 0.0).astype(BF16)
            sent(at).start()

    @pl.when(row > col)
    def _():
        held[:480] = jnp.zeros((480, columns), BF16)
        for at, (first, end) in enumerate(BLOCKS):
            sent(at, held.at[: end - first]).start()

    for at in range(len(BLOCKS)):
        sent(at).wait()


def per_device(residual, interaction, commands, slope_valid, frame_valid):
    rows, width = interaction.shape
    row, col = lax.axis_index("row"), lax.axis_index("col")
    at = jnp.stack([row, col]).astype(jnp.int32)
    limit = pltpu.CompilerParams(vmem_limit_bytes=48 * 1024 * 1024)
    call = functools.partial(pl.pallas_call, compiler_params=limit)
    turned = interaction.T
    sent_a, sent_b, ordered = call(
        first_kernel,
        out_shape=(shape(128, rows), shape(128, rows), shape(256, width)),
        in_specs=[SCALAR, WHOLE, WHOLE],
        out_specs=(WHOLE, WHOLE, WHOLE),
        cost_estimate=pl.CostEstimate(
            flops=2 * 256 * width * rows, bytes_accessed=1600000, transcendentals=0
        ),
    )(at, commands, turned)
    got_a = lax.ppermute(sent_a, "col", y_swap(1))
    got_b = lax.ppermute(sent_b, "col", y_swap(3))
    kept_a, kept_b = call(
        second_kernel,
        out_shape=(shape(128, rows), shape(128, rows)),
        in_specs=[WHOLE, WHOLE],
        out_specs=(WHOLE, WHOLE),
        cost_estimate=pl.CostEstimate(
            flops=2 * 256 * width * rows, bytes_accessed=1600000, transcendentals=0
        ),
    )(ordered, turned)
    for swap_a, swap_b in (
        (y_swap(3), y_swap(1)),
        (z_swap(1), z_swap(3)),
        (z_swap(3), z_swap(1)),
    ):
        half = kept_a.shape[0] // 2
        sent_a, sent_b = add(kept_a[half:], got_a[half:]), add(kept_b[half:], got_b[half:])
        next_a = lax.ppermute(sent_a, "col", swap_a)
        next_b = lax.ppermute(sent_b, "col", swap_b)
        kept_a, kept_b = add(kept_a[:half], got_a[:half]), add(kept_b[:half], got_b[:half])
        got_a, got_b = next_a, next_b
    summed = jnp.concatenate([kept_a, kept_b]).astype(F32) + jnp.concatenate(
        [got_a, got_b]
    ).astype(F32)
    row_mask = jnp.broadcast_to(slope_valid[:, None], (rows // SBLK, SBLK)).reshape(-1)
    slopes = (
        (residual.T.astype(F32) + summed)
        * row_mask[None, :].astype(F32)
        * frame_valid[:, None].astype(F32)
    ).astype(BF16)

    def halves(one, two, flops):
        half = one.shape[0] // 2
        return call(
            halves_kernel,
            out_shape=(shape(half, rows),) * 2,
            in_specs=[WHOLE] * 2,
            out_specs=(WHOLE,) * 2,
            cost_estimate=pl.CostEstimate(flops=flops, bytes_accessed=983040, transcendentals=0),
        )(one, two)

    left = lax.ppermute(slopes, "col", z_turn(1))
    right = lax.ppermute(slopes, "col", z_turn(-1))
    flipped = lax.ppermute(slopes, ("row", "col"), flip_pairs())
    far = lax.ppermute(slopes, "col", z_turn(2))
    mine = call(
        z_join_kernel,
        out_shape=shape(128, rows),
        in_specs=[SCALAR] + [WHOLE] * 4,
        out_specs=WHOLE,
        cost_estimate=pl.CostEstimate(flops=4000000000, bytes_accessed=983040, transcendentals=0),
    )(at, slopes, right, left, far)
    left = lax.ppermute(mine, "col", y_turn(1))
    right = lax.ppermute(mine, "col", y_turn(-1))
    pair = lax.ppermute(flipped, "row", [(r, r ^ 8) for r in range(16)])
    near = call(
        pair_join_kernel,
        out_shape=shape(64, rows),
        in_specs=[SCALAR] + [WHOLE] * 2,
        out_specs=WHOLE,
        cost_estimate=pl.CostEstimate(flops=0, bytes_accessed=491520, transcendentals=0),
    )(at, flipped, pair)
    x_left = lax.ppermute(near, "row", x_turn(1))
    x_right = lax.ppermute(near, "row", x_turn(-1))
    low, high = halves(left, right, 8000000000)
    far_a = lax.ppermute(low, "col", y_turn(1))
    far_b = lax.ppermute(high, "col", y_turn(-1))
    far = call(
        stack_kernel,
        out_shape=shape(128, rows),
        in_specs=[WHOLE] * 2,
        out_specs=WHOLE,
        cost_estimate=pl.CostEstimate(flops=8000000000, bytes_accessed=983040, transcendentals=0),
    )(far_a, far_b)
    x_low, x_high = halves(x_left, x_right, 0)
    x_far_a = lax.ppermute(x_low, "row", x_turn(1))
    x_far_b = lax.ppermute(x_high, "row", x_turn(-1))
    near = call(
        gather_kernel, out_shape=shape(256, rows), in_specs=[WHOLE] * 6, out_specs=WHOLE
    )(near, x_left, x_right, x_far_a, x_far_b, low)
    other = lax.ppermute(near, "row", [(r, r ^ 1) for r in range(16)])
    return call(
        last_kernel,
        out_shape=shape(rows, rows),
        in_specs=[SCALAR] + [WHOLE] * 6,
        out_specs=pl.BlockSpec(memory_space=pl.ANY),
        scratch_shapes=[
            pltpu.VMEM((FRAMES, rows), BF16),
            pltpu.VMEM((FRAMES, rows), BF16),
            pltpu.VMEM((rows, rows), BF16),
            pltpu.SemaphoreType.DMA((len(BLOCKS),)),
        ],
        cost_estimate=pl.CostEstimate(
            flops=2 * FRAMES * rows * rows, bytes_accessed=2 * rows * rows, transcendentals=0
        ),
    )(at, mine, left, right, far, near, other)


def solution(mesh):
    placed = (P("row", "col"), P("row", "col"), P("col", None), P("row"), P("col"))
    return jax.shard_map(
        per_device, mesh=mesh, in_specs=placed, out_specs=P("row", "col"), check_vma=False
    )
```

```python
import functools

import jax
import jax.numpy as jnp
from jax import lax
from jax.experimental import pallas as pl
from jax.experimental.pallas import tpu as pltpu
from jax.sharding import PartitionSpec as P

SBLK = 128
FRAMES = 512
BF16 = jnp.bfloat16
F32 = jnp.float32
WHOLE = pl.BlockSpec(memory_space=pltpu.VMEM)
SCALAR = pl.BlockSpec(memory_space=pltpu.SMEM)


def y_swap(mask):
    return [(c, c ^ mask) for c in range(16)]


def z_swap(mask):
    return [(c, c ^ (4 * mask)) for c in range(16)]


def y_turn(by):
    return [(c, (c & 12) | ((c + by) & 3)) for c in range(16)]


def z_turn(by):
    return [(c, (c + 4 * by) & 15) for c in range(16)]


def x_turn(by):
    return [(r, (r & 9) | ((r + 2 * by) & 6)) for r in range(16)]


def flip_pairs():
    pairs = []
    for r in range(16):
        for c in range(16):
            z_hi, y = c >> 2, c & 3
            x = (((r >> 1) & 3) + y) & 3
            to = (z_hi >> 1) * 8 + x * 2 + (z_hi & 1)
            pairs.append((r * 16 + c, to * 16 + r))
    return pairs


def add(one, other):
    return (one.astype(F32) + other.astype(F32)).astype(BF16)


def shape(rows, cols):
    return jax.ShapeDtypeStruct((rows, cols), BF16)


def first_kernel(at_ref, commands_ref, interaction_ref, sent_a, sent_b, ordered_ref):
    col = at_ref[1]
    out = lax.broadcasted_iota(jnp.int32, (FRAMES, FRAMES), 0)
    src = lax.broadcasted_iota(jnp.int32, (FRAMES, FRAMES), 1)
    half = out >> 8
    low = out & 15

    def mask_of(at):
        one, two = at & 1, at >> 1
        return jnp.where(half == 0, (one << 1) | (one ^ two), at ^ two)

    piece = col ^ (mask_of((out >> 6) & 3) + 4 * mask_of((out >> 4) & 3))
    pick = (src == piece * 32 + half * 16 + low).astype(F32).astype(BF16)
    ordered = lax.dot_general(
        pick, commands_ref[...], (((1,), (1,)), ((), ())), preferred_element_type=F32
    ).astype(BF16)
    sent_a[...] = jnp.dot(
        ordered[128:256], interaction_ref[...], preferred_element_type=F32
    ).astype(BF16)
    sent_b[...] = jnp.dot(
        ordered[384:512], interaction_ref[...], preferred_element_type=F32
    ).astype(BF16)
    ordered_ref[:128] = ordered[:128]
    ordered_ref[128:] = ordered[256:384]


def second_kernel(ordered_ref, interaction_ref, kept_a, kept_b):
    kept_a[...] = jnp.dot(
        ordered_ref[:128], interaction_ref[...], preferred_element_type=F32
    ).astype(BF16)
    kept_b[...] = jnp.dot(
        ordered_ref[128:], interaction_ref[...], preferred_element_type=F32
    ).astype(BF16)


def halves_kernel(left, right, low, high):
    half = low.shape[0]
    low[...] = left[:half]
    high[...] = right[half:]


def z_join_kernel(at_ref, own, right, left, far, mine):
    z = at_ref[1] >> 2
    for by, ref in ((0, own), (3, left), (1, right), (2, far)):
        mine[pl.ds(pl.multiple_of(((z + by) & 3) * 32, 32), 32)] = ref[...]


def pair_join_kernel(at_ref, flipped, pair, near):
    z_lo = at_ref[0] >> 3
    near[pl.ds(pl.multiple_of(z_lo * 32, 32), 32)] = flipped[...]
    near[pl.ds(pl.multiple_of((1 - z_lo) * 32, 32), 32)] = pair[...]


def gather_kernel(near, x_left, x_right, x_far_a, x_far_b, after, out):
    first = 0
    for ref in (near, x_left, x_right, x_far_a, x_far_b):
        out[first : first + ref.shape[0]] = ref[...]
        first += ref.shape[0]


def stack_kernel(one, two, out):
    half = one.shape[0]
    out[:half] = one[...]
    out[half:] = two[...]


BLOCKS = ((0, 480), (480, 960), (960, 1440), (1440, 1760), (1760, 1920))


def last_kernel(
    at_ref,
    own,
    left,
    right,
    far,
    near,
    other,
    out,
    lhs,
    rhs,
    held,
    done,
):
    row, col = at_ref[0], at_ref[1]
    columns = held.shape[1]
    dims = (((0,), (0,)), ((), ()))

    def sent(at, source=None):
        first, end = BLOCKS[at]
        source = held.at[first:end] if source is None else source
        return pltpu.make_async_copy(source, out.at[first:end], done.at[at])

    @pl.when(row <= col)
    def _():
        y = col & 3

        for by, ref in ((0, own), (3, left), (1, right), (2, far)):
            lhs[pl.ds(pl.multiple_of(((y + by) & 3) * 128, 128), 128)] = ref[...]
        x, core = (row >> 1) & 3, row & 1
        for swap, ref in ((0, near), (1, other)):
            for at, by in enumerate((0, 3, 1, 2)):
                y_from = (x + by - (col >> 1)) & 3
                for z_lo in range(2):
                    z_from = z_lo * 2 + (core ^ swap)
                    first = pl.multiple_of(y_from * 128 + z_from * 32, 32)
                    rhs[pl.ds(first, 32)] = ref[at * 64 + z_lo * 32 : at * 64 + z_lo * 32 + 32]

    @pl.when(row < col)
    def _():
        for at, (first, end) in enumerate(BLOCKS):
            tile = lax.dot_general(lhs[:, first:end], rhs[...], dims, preferred_element_type=F32)
            held[first:end] = (tile * (1.0 / FRAMES)).astype(BF16)
            sent(at).start()

    @pl.when(row == col)
    def _():
        for at, (first, end) in enumerate(BLOCKS):
            low = first // 128 * 128
            if low:
                held[first:end, :low] = jnp.zeros((end - first, low), BF16)
            tile = lax.dot_general(
                lhs[:, first:end], rhs[:, low:], dims, preferred_element_type=F32
            ) * (1.0 / FRAMES)
            down = lax.broadcasted_iota(jnp.int32, tile.shape, 0) + first
            across = lax.broadcasted_iota(jnp.int32, tile.shape, 1) + low
            held[first:end, low:] = jnp.where(down <= across, tile, 0.0).astype(BF16)
            sent(at).start()

    @pl.when(row > col)
    def _():
        held[:480] = jnp.zeros((480, columns), BF16)
        for at, (first, end) in enumerate(BLOCKS):
            sent(at, held.at[: end - first]).start()

    for at in range(len(BLOCKS)):
        sent(at).wait()


def per_device(residual, interaction, commands, slope_valid, frame_valid):
    rows, width = interaction.shape
    row, col = lax.axis_index("row"), lax.axis_index("col")
    at = jnp.stack([row, col]).astype(jnp.int32)
    limit = pltpu.CompilerParams(vmem_limit_bytes=48 * 1024 * 1024)
    call = functools.partial(pl.pallas_call, compiler_params=limit)
    turned = interaction.T
    sent_a, sent_b, ordered = call(
        first_kernel,
        out_shape=(shape(128, rows), shape(128, rows), shape(256, width)),
        in_specs=[SCALAR, WHOLE, WHOLE],
        out_specs=(WHOLE, WHOLE, WHOLE),
        cost_estimate=pl.CostEstimate(
            flops=2 * 256 * width * rows, bytes_accessed=1600000, transcendentals=0
        ),
    )(at, commands, turned)
    got_a = lax.ppermute(sent_a, "col", y_swap(1))
    got_b = lax.ppermute(sent_b, "col", y_swap(3))
    kept_a, kept_b = call(
        second_kernel,
        out_shape=(shape(128, rows), shape(128, rows)),
        in_specs=[WHOLE, WHOLE],
        out_specs=(WHOLE, WHOLE),
        cost_estimate=pl.CostEstimate(
            flops=2 * 256 * width * rows, bytes_accessed=1600000, transcendentals=0
        ),
    )(ordered, turned)
    for swap_a, swap_b in (
        (y_swap(3), y_swap(1)),
        (z_swap(1), z_swap(3)),
        (z_swap(3), z_swap(1)),
    ):
        half = kept_a.shape[0] // 2
        sent_a, sent_b = add(kept_a[half:], got_a[half:]), add(kept_b[half:], got_b[half:])
        next_a = lax.ppermute(sent_a, "col", swap_a)
        next_b = lax.ppermute(sent_b, "col", swap_b)
        kept_a, kept_b = add(kept_a[:half], got_a[:half]), add(kept_b[:half], got_b[:half])
        got_a, got_b = next_a, next_b
    summed = jnp.concatenate([kept_a, kept_b]).astype(F32) + jnp.concatenate(
        [got_a, got_b]
    ).astype(F32)
    row_mask = jnp.broadcast_to(slope_valid[:, None], (rows // SBLK, SBLK)).reshape(-1)
    slopes = (
        (residual.T.astype(F32) + summed)
        * row_mask[None, :].astype(F32)
        * frame_valid[:, None].astype(F32)
    ).astype(BF16)

    def halves(one, two, flops):
        half = one.shape[0] // 2
        return call(
            halves_kernel,
            out_shape=(shape(half, rows),) * 2,
            in_specs=[WHOLE] * 2,
            out_specs=(WHOLE,) * 2,
            cost_estimate=pl.CostEstimate(flops=flops, bytes_accessed=983040, transcendentals=0),
        )(one, two)

    left = lax.ppermute(slopes, "col", z_turn(1))
    right = lax.ppermute(slopes, "col", z_turn(-1))
    flipped = lax.ppermute(slopes, ("row", "col"), flip_pairs())
    far = lax.ppermute(slopes, "col", z_turn(2))
    mine = call(
        z_join_kernel,
        out_shape=shape(128, rows),
        in_specs=[SCALAR] + [WHOLE] * 4,
        out_specs=WHOLE,
        cost_estimate=pl.CostEstimate(flops=4000000000, bytes_accessed=983040, transcendentals=0),
    )(at, slopes, right, left, far)
    left = lax.ppermute(mine, "col", y_turn(1))
    right = lax.ppermute(mine, "col", y_turn(-1))
    pair = lax.ppermute(flipped, "row", [(r, r ^ 8) for r in range(16)])
    near = call(
        pair_join_kernel,
        out_shape=shape(64, rows),
        in_specs=[SCALAR] + [WHOLE] * 2,
        out_specs=WHOLE,
        cost_estimate=pl.CostEstimate(flops=3000000000, bytes_accessed=491520, transcendentals=0),
    )(at, flipped, pair)
    x_left = lax.ppermute(near, "row", x_turn(1))
    x_right = lax.ppermute(near, "row", x_turn(-1))
    low, high = halves(left, right, 16000000000)
    far_a = lax.ppermute(low, "col", y_turn(1))
    far_b = lax.ppermute(high, "col", y_turn(-1))
    far = call(
        stack_kernel,
        out_shape=shape(128, rows),
        in_specs=[WHOLE] * 2,
        out_specs=WHOLE,
        cost_estimate=pl.CostEstimate(flops=30000000000, bytes_accessed=983040, transcendentals=0),
    )(far_a, far_b)
    x_low, x_high = halves(x_left, x_right, 0)
    x_far_a = lax.ppermute(x_low, "row", x_turn(1))
    x_far_b = lax.ppermute(x_high, "row", x_turn(-1))
    near = call(
        gather_kernel, out_shape=shape(256, rows), in_specs=[WHOLE] * 6, out_specs=WHOLE
    )(near, x_left, x_right, x_far_a, x_far_b, low)
    other = lax.ppermute(near, "row", [(r, r ^ 1) for r in range(16)])
    return call(
        last_kernel,
        out_shape=shape(rows, rows),
        in_specs=[SCALAR] + [WHOLE] * 6,
        out_specs=pl.BlockSpec(memory_space=pl.ANY),
        scratch_shapes=[
            pltpu.VMEM((FRAMES, rows), BF16),
            pltpu.VMEM((FRAMES, rows), BF16),
            pltpu.VMEM((rows, rows), BF16),
            pltpu.SemaphoreType.DMA((len(BLOCKS),)),
        ],
        cost_estimate=pl.CostEstimate(
            flops=2 * FRAMES * rows * rows, bytes_accessed=2 * rows * rows, transcendentals=0
        ),
    )(at, mine, left, right, far, near, other)


def solution(mesh):
    placed = (P("row", "col"), P("row", "col"), P("col", None), P("row"), P("col"))
    return jax.shard_map(
        per_device, mesh=mesh, in_specs=placed, out_specs=P("row", "col"), check_vma=False
    )
```

```python
import functools

import jax
import jax.numpy as jnp
from jax import lax
from jax.experimental import pallas as pl
from jax.experimental.pallas import tpu as pltpu
from jax.sharding import PartitionSpec as P

SBLK = 128
FRAMES = 512
BF16 = jnp.bfloat16
F32 = jnp.float32
WHOLE = pl.BlockSpec(memory_space=pltpu.VMEM)
SCALAR = pl.BlockSpec(memory_space=pltpu.SMEM)


def y_swap(mask):
    return [(c, c ^ mask) for c in range(16)]


def z_swap(mask):
    return [(c, c ^ (4 * mask)) for c in range(16)]


def y_turn(by):
    return [(c, (c & 12) | ((c + by) & 3)) for c in range(16)]


def z_turn(by):
    return [(c, (c + 4 * by) & 15) for c in range(16)]


def x_turn(by):
    return [(r, (r & 9) | ((r + 2 * by) & 6)) for r in range(16)]


def flip_pairs():
    pairs = []
    for r in range(16):
        for c in range(16):
            z_hi, y = c >> 2, c & 3
            x = (((r >> 1) & 3) + y) & 3
            to = (z_hi >> 1) * 8 + x * 2 + (z_hi & 1)
            pairs.append((r * 16 + c, to * 16 + r))
    return pairs


def add(one, other):
    return (one.astype(F32) + other.astype(F32)).astype(BF16)


def shape(rows, cols):
    return jax.ShapeDtypeStruct((rows, cols), BF16)


def first_kernel(at_ref, commands_ref, interaction_ref, sent_a, sent_b, ordered_ref):
    col = at_ref[1]
    out = lax.broadcasted_iota(jnp.int32, (FRAMES, FRAMES), 0)
    src = lax.broadcasted_iota(jnp.int32, (FRAMES, FRAMES), 1)
    half = out >> 8
    low = out & 15

    def mask_of(at):
        one, two = at & 1, at >> 1
        return jnp.where(half == 0, (one << 1) | (one ^ two), at ^ two)

    piece = col ^ (mask_of((out >> 6) & 3) + 4 * mask_of((out >> 4) & 3))
    pick = (src == piece * 32 + half * 16 + low).astype(F32).astype(BF16)
    ordered = lax.dot_general(
        pick, commands_ref[...], (((1,), (1,)), ((), ())), preferred_element_type=F32
    ).astype(BF16)
    sent_a[...] = jnp.dot(
        ordered[128:256], interaction_ref[...], preferred_element_type=F32
    ).astype(BF16)
    sent_b[...] = jnp.dot(
        ordered[384:512], interaction_ref[...], preferred_element_type=F32
    ).astype(BF16)
    ordered_ref[:128] = ordered[:128]
    ordered_ref[128:] = ordered[256:384]


def second_kernel(ordered_ref, interaction_ref, kept_a, kept_b):
    kept_a[...] = jnp.dot(
        ordered_ref[:128], interaction_ref[...], preferred_element_type=F32
    ).astype(BF16)
    kept_b[...] = jnp.dot(
        ordered_ref[128:], interaction_ref[...], preferred_element_type=F32
    ).astype(BF16)


def halves_kernel(left, right, low, high):
    half = low.shape[0]
    low[...] = left[:half]
    high[...] = right[half:]


def z_join_kernel(at_ref, own, right, left, far, mine):
    z = at_ref[1] >> 2
    for by, ref in ((0, own), (3, left), (1, right), (2, far)):
        mine[pl.ds(pl.multiple_of(((z + by) & 3) * 32, 32), 32)] = ref[...]


def pair_join_kernel(at_ref, flipped, pair, near):
    z_lo = at_ref[0] >> 3
    near[pl.ds(pl.multiple_of(z_lo * 32, 32), 32)] = flipped[...]
    near[pl.ds(pl.multiple_of((1 - z_lo) * 32, 32), 32)] = pair[...]


def gather_kernel(near, x_left, x_right, x_far_a, x_far_b, after, out):
    first = 0
    for ref in (near, x_left, x_right, x_far_a, x_far_b):
        out[first : first + ref.shape[0]] = ref[...]
        first += ref.shape[0]


def stack_kernel(one, two, out):
    half = one.shape[0]
    out[:half] = one[...]
    out[half:] = two[...]


BLOCKS = ((0, 640), (640, 1280), (1280, 1792), (1792, 1920))


def last_kernel(
    at_ref,
    own,
    left,
    right,
    far,
    near,
    other,
    out,
    lhs,
    rhs,
    held,
    done,
):
    row, col = at_ref[0], at_ref[1]
    columns = held.shape[1]
    dims = (((0,), (0,)), ((), ()))

    def sent(at, source=None):
        first, end = BLOCKS[at]
        source = held.at[first:end] if source is None else source
        return pltpu.make_async_copy(source, out.at[first:end], done.at[at])

    @pl.when(row <= col)
    def _():
        y = col & 3

        for by, ref in ((0, own), (3, left), (1, right), (2, far)):
            lhs[pl.ds(pl.multiple_of(((y + by) & 3) * 128, 128), 128)] = ref[...]
        x, core = (row >> 1) & 3, row & 1
        for swap, ref in ((0, near), (1, other)):
            for at, by in enumerate((0, 3, 1, 2)):
                y_from = (x + by - (col >> 1)) & 3
                for z_lo in range(2):
                    z_from = z_lo * 2 + (core ^ swap)
                    first = pl.multiple_of(y_from * 128 + z_from * 32, 32)
                    rhs[pl.ds(first, 32)] = ref[at * 64 + z_lo * 32 : at * 64 + z_lo * 32 + 32]

    @pl.when(row < col)
    def _():
        for at, (first, end) in enumerate(BLOCKS):
            tile = lax.dot_general(lhs[:, first:end], rhs[...], dims, preferred_element_type=F32)
            held[first:end] = (tile * (1.0 / FRAMES)).astype(BF16)
            sent(at).start()

    @pl.when(row == col)
    def _():
        for at, (first, end) in enumerate(BLOCKS):
            low = first // 128 * 128
            if low:
                held[first:end, :low] = jnp.zeros((end - first, low), BF16)
            tile = lax.dot_general(
                lhs[:, first:end], rhs[:, low:], dims, preferred_element_type=F32
            ) * (1.0 / FRAMES)
            down = lax.broadcasted_iota(jnp.int32, tile.shape, 0) + first
            across = lax.broadcasted_iota(jnp.int32, tile.shape, 1) + low
            held[first:end, low:] = jnp.where(down <= across, tile, 0.0).astype(BF16)
            sent(at).start()

    @pl.when(row > col)
    def _():
        held[:640] = jnp.zeros((640, columns), BF16)
        for at, (first, end) in enumerate(BLOCKS):
            sent(at, held.at[: end - first]).start()

    for at in range(len(BLOCKS)):
        sent(at).wait()


def per_device(residual, interaction, commands, slope_valid, frame_valid):
    rows, width = interaction.shape
    row, col = lax.axis_index("row"), lax.axis_index("col")
    at = jnp.stack([row, col]).astype(jnp.int32)
    limit = pltpu.CompilerParams(vmem_limit_bytes=48 * 1024 * 1024)
    call = functools.partial(pl.pallas_call, compiler_params=limit)
    turned = interaction.T
    sent_a, sent_b, ordered = call(
        first_kernel,
        out_shape=(shape(128, rows), shape(128, rows), shape(256, width)),
        in_specs=[SCALAR, WHOLE, WHOLE],
        out_specs=(WHOLE, WHOLE, WHOLE),
        cost_estimate=pl.CostEstimate(
            flops=2 * 256 * width * rows, bytes_accessed=1600000, transcendentals=0
        ),
    )(at, commands, turned)
    got_a = lax.ppermute(sent_a, "col", y_swap(1))
    got_b = lax.ppermute(sent_b, "col", y_swap(3))
    kept_a, kept_b = call(
        second_kernel,
        out_shape=(shape(128, rows), shape(128, rows)),
        in_specs=[WHOLE, WHOLE],
        out_specs=(WHOLE, WHOLE),
        cost_estimate=pl.CostEstimate(
            flops=2 * 256 * width * rows, bytes_accessed=1600000, transcendentals=0
        ),
    )(ordered, turned)
    for swap_a, swap_b in (
        (y_swap(3), y_swap(1)),
        (z_swap(1), z_swap(3)),
        (z_swap(3), z_swap(1)),
    ):
        half = kept_a.shape[0] // 2
        sent_a, sent_b = add(kept_a[half:], got_a[half:]), add(kept_b[half:], got_b[half:])
        next_a = lax.ppermute(sent_a, "col", swap_a)
        next_b = lax.ppermute(sent_b, "col", swap_b)
        kept_a, kept_b = add(kept_a[:half], got_a[:half]), add(kept_b[:half], got_b[:half])
        got_a, got_b = next_a, next_b
    summed = jnp.concatenate([kept_a, kept_b]).astype(F32) + jnp.concatenate(
        [got_a, got_b]
    ).astype(F32)
    row_mask = jnp.broadcast_to(slope_valid[:, None], (rows // SBLK, SBLK)).reshape(-1)
    slopes = (
        (residual.T.astype(F32) + summed)
        * row_mask[None, :].astype(F32)
        * frame_valid[:, None].astype(F32)
    ).astype(BF16)

    def halves(one, two, flops):
        half = one.shape[0] // 2
        return call(
            halves_kernel,
            out_shape=(shape(half, rows),) * 2,
            in_specs=[WHOLE] * 2,
            out_specs=(WHOLE,) * 2,
            cost_estimate=pl.CostEstimate(flops=flops, bytes_accessed=983040, transcendentals=0),
        )(one, two)

    left = lax.ppermute(slopes, "col", z_turn(1))
    right = lax.ppermute(slopes, "col", z_turn(-1))
    flipped = lax.ppermute(slopes, ("row", "col"), flip_pairs())
    far = lax.ppermute(slopes, "col", z_turn(2))
    mine = call(
        z_join_kernel,
        out_shape=shape(128, rows),
        in_specs=[SCALAR] + [WHOLE] * 4,
        out_specs=WHOLE,
        cost_estimate=pl.CostEstimate(flops=4000000000, bytes_accessed=983040, transcendentals=0),
    )(at, slopes, right, left, far)
    left = lax.ppermute(mine, "col", y_turn(1))
    right = lax.ppermute(mine, "col", y_turn(-1))
    pair = lax.ppermute(flipped, "row", [(r, r ^ 8) for r in range(16)])
    near = call(
        pair_join_kernel,
        out_shape=shape(64, rows),
        in_specs=[SCALAR] + [WHOLE] * 2,
        out_specs=WHOLE,
        cost_estimate=pl.CostEstimate(flops=3000000000, bytes_accessed=491520, transcendentals=0),
    )(at, flipped, pair)
    x_left = lax.ppermute(near, "row", x_turn(1))
    x_right = lax.ppermute(near, "row", x_turn(-1))
    low, high = halves(left, right, 16000000000)
    far_a = lax.ppermute(low, "col", y_turn(1))
    far_b = lax.ppermute(high, "col", y_turn(-1))
    far = call(
        stack_kernel,
        out_shape=shape(128, rows),
        in_specs=[WHOLE] * 2,
        out_specs=WHOLE,
        cost_estimate=pl.CostEstimate(flops=30000000000, bytes_accessed=983040, transcendentals=0),
    )(far_a, far_b)
    x_low, x_high = halves(x_left, x_right, 0)
    x_far_a = lax.ppermute(x_low, "row", x_turn(1))
    x_far_b = lax.ppermute(x_high, "row", x_turn(-1))
    near = call(
        gather_kernel, out_shape=shape(256, rows), in_specs=[WHOLE] * 6, out_specs=WHOLE
    )(near, x_left, x_right, x_far_a, x_far_b, low)
    other = lax.ppermute(near, "row", [(r, r ^ 1) for r in range(16)])
    return call(
        last_kernel,
        out_shape=shape(rows, rows),
        in_specs=[SCALAR] + [WHOLE] * 6,
        out_specs=pl.BlockSpec(memory_space=pl.ANY),
        scratch_shapes=[
            pltpu.VMEM((FRAMES, rows), BF16),
            pltpu.VMEM((FRAMES, rows), BF16),
            pltpu.VMEM((rows, rows), BF16),
            pltpu.SemaphoreType.DMA((len(BLOCKS),)),
        ],
        cost_estimate=pl.CostEstimate(
            flops=2 * FRAMES * rows * rows, bytes_accessed=2 * rows * rows, transcendentals=0
        ),
    )(at, mine, left, right, far, near, other)


def solution(mesh):
    placed = (P("row", "col"), P("row", "col"), P("col", None), P("row"), P("col"))
    return jax.shard_map(
        per_device, mesh=mesh, in_specs=placed, out_specs=P("row", "col"), check_vma=False
    )
```
